32 devices in a mesh: row: 4 (over y, x), mode: 8 (over z, core).
Axes of the slice: x: 2, y: 2, z: 4, core: 2. Of those that a mesh axis runs over, the one named last changes fastest.
Arguments:
- transfer_matrix: float32 [2, 768, 49152], P(None, 'row', 'mode'), may hold values from -0.01953125 to 0.01953125
- probes: float32 [2, 49152, 256], P(None, ('mode', 'row')), may hold values from -6 to 6
- intensity: float32 [768, 256], P('row'), may hold values from 0.25 to 4
Outputs:
- gradient: float32 [2, 768, 49152], P(None, 'row', 'mode')
The draws below stay inside these ranges and needn't reach their ends.
All inputs are finite; a program needn't handle non-finite values.
Results may differ from the reference program's by a relative error of at most 0.00012.
Values sent between devices are 32-bit elements; how exact they have to be, the bound alone decides.
No kernel may reach another device: no remote copies, remote signals or barrier semaphores. Data moves between devices by JAX's collectives and lax.ppermute only.
A program may use at most 64 MiB of HBM per device.

```python
import math
import jax
import jax.numpy as jnp
from jax import lax

N = 49152
P_SIZE = 256
M = 768


def block_levels(own_key, extent, cuts, low, high):
    loudness = 1.0
    for dim, blocks in cuts:
        draws = jax.random.uniform(jax.random.fold_in(jax.random.fold_in(own_key, 6), dim), (blocks,), jnp.float32, low / len(cuts), high / len(cuts))
        loudness = loudness * jnp.repeat(jnp.exp(draws), extent[dim] // blocks).reshape((-1,) + (1,) * (len(extent) - 1 - dim))
    return loudness


def centred(rng, shape, scale, limit, split=(), held_as=jnp.bfloat16):
    values = scale * jax.random.normal(rng, shape, jnp.float32)
    if split:
        values = values * block_levels(rng, shape, split, -0.22, 0.18)
    return jnp.clip(values, -limit, limit).astype(held_as)


def setup_inputs(seed: int = 0) -> dict:
    streams_of = jax.random.split(jax.random.key(seed), 4)
    transfer_matrix = centred(streams_of[0], (2, M, N), (2 * N) ** -0.5, 0.01953125, ((1, 4), (2, 8)), jnp.float32)
    probes = centred(streams_of[1], (2, N, P_SIZE), 1.0, 6.0, ((1, 32),), jnp.float32)
    intensity = jnp.clip(jnp.exp(math.log(4.0) - 2.7725887 * jax.random.uniform(streams_of[2], (M, P_SIZE), jnp.float32) ** block_levels(streams_of[2], (M, P_SIZE), ((0, 4),), -0.2, 0.2)), 0.25, 4.0)
    return dict(transfer_matrix=transfer_matrix, probes=probes, intensity=intensity)


def exact_dot(left, right):
    return jnp.dot(left, right, precision=lax.Precision.HIGHEST, preferred_element_type=jnp.float32)


def exact_dot_transposed(left, right):
    return lax.dot_general(left, right, (((1,), (1,)), ((), ())), precision=lax.Precision.HIGHEST, preferred_element_type=jnp.float32)


def reference(transfer_matrix, probes, intensity):
    fields_real = exact_dot(transfer_matrix[0], probes[0]) - exact_dot(transfer_matrix[1], probes[1])
    fields_imag = exact_dot(transfer_matrix[0], probes[1]) + exact_dot(transfer_matrix[1], probes[0])
    excess = fields_real * fields_real + fields_imag * fields_imag - intensity
    resid_real = excess * fields_real / P_SIZE
    resid_imag = excess * fields_imag / P_SIZE
    grad_real = exact_dot_transposed(resid_real, probes[0]) + exact_dot_transposed(resid_imag, probes[1])
    grad_imag = exact_dot_transposed(resid_imag, probes[0]) - exact_dot_transposed(resid_real, probes[1])
    return jnp.stack([grad_real, grad_imag])
```

```python
import functools

import jax
import jax.numpy as jnp
from jax import lax
from jax.experimental import pallas as pl
from jax.experimental.pallas import tpu as pltpu
from jax.sharding import PartitionSpec as P

LANES = 128
LAST_PROBES = 64
MIB = 1024 * 1024
VMEM = pl.BlockSpec(memory_space=pltpu.VMEM)
SMEM = pl.BlockSpec(memory_space=pltpu.SMEM)
COST = pl.CostEstimate(flops=1000, bytes_accessed=1000, transcendentals=0)


def halves(value):
    high = value.astype(jnp.bfloat16)
    return high, (value - high.astype(jnp.float32)).astype(jnp.bfloat16)


def dot(left, right, dimension=0):
    return lax.dot_general(
        left, right, (((1,), (dimension,)), ((), ())), preferred_element_type=jnp.float32
    )


def params(mib):
    return pltpu.CompilerParams(vmem_limit_bytes=mib * MIB)


def in_order(value, *earlier):
    return lax.optimization_barrier((value, *earlier))[0]


def groups(low, high):
    cuts = [low, *range(low // LANES * LANES + LANES, high, LANES), high]
    return list(zip(cuts, cuts[1:]))


def group_widths(low, high):
    return [end - start for start, end in groups(low, high)]


def chunk_kernel(low, high, probes_ref, *refs):
    outs, (slots_ref, done_ref, slot_done_ref) = refs[:2], refs[2:]
    half = outs[0].shape[0]
    copies, later = [], []
    for which, out_ref in enumerate(outs):
        place = 0
        modes = pl.ds(which * half, half)
        for start, end in groups(low, high):
            block = pl.ds(start // LANES * LANES, LANES)
            for part in range(2):
                if end - start == LANES:
                    target = out_ref.at[:, pl.ds(place + part * LANES, LANES)]
                    copy = pltpu.make_async_copy(
                        probes_ref.at[part, modes, block], target, done_ref.at[len(copies)]
                    )
                    copies.append(copy)
                else:
                    slot = 2 * which + part
                    copy = pltpu.make_async_copy(
                        probes_ref.at[part, modes, block], slots_ref.at[slot], slot_done_ref.at[slot]
                    )
                    later.append((copy, out_ref, slot, place + part * (end - start), start, end))
                copy.start()
            place += 2 * (end - start)
    for copy, out_ref, slot, place, start, end in later:
        copy.wait()
        first = start % LANES
        out_ref[:, place : place + end - start] = slots_ref[slot, :, first : first + end - start]
    for copy in copies:
        copy.wait()


def probe_chunk(probes, low, high):
    half, width = probes.shape[1] // 2, high - low
    whole = sum(size == LANES for size in group_widths(low, high))
    return pl.pallas_call(
        functools.partial(chunk_kernel, low, high),
        in_specs=[pl.BlockSpec(memory_space=pl.ANY)],
        out_specs=[VMEM, VMEM],
        out_shape=[jax.ShapeDtypeStruct((half, 2 * width), jnp.float32)] * 2,
        scratch_shapes=[
            pltpu.VMEM((4, half, LANES), jnp.float32),
            pltpu.SemaphoreType.DMA((max(4 * whole, 1),)),
            pltpu.SemaphoreType.DMA((4,)),
        ],
        compiler_params=params(8),
        cost_estimate=COST,
    )(probes)


def matrix_kernel(order_ref, matrix_ref, high_ref, low_ref):
    high_ref[...], low_ref[...] = halves(matrix_ref[...].reshape(high_ref.shape))


def matrix_halves(matrix, order, half):
    _, rows, modes = matrix.shape
    out = jax.ShapeDtypeStruct((2 * rows, modes), jnp.bfloat16)
    spec = pl.BlockSpec((2 * rows, half), lambda i, _: (0, i))
    return pl.pallas_call(
        matrix_kernel,
        grid_spec=pltpu.PrefetchScalarGridSpec(
            num_scalar_prefetch=1,
            grid=(modes // half,),
            in_specs=[pl.BlockSpec((2, rows, half), lambda i, order_ref: (0, 0, order_ref[i]))],
            out_specs=[spec, spec],
        ),
        out_shape=[out, out],
        compiler_params=params(12),
        cost_estimate=COST,
    )(order, matrix)


def packed_shape(rows, width):
    return rows * width // LANES, LANES


def packed(value):
    rows, width = value.shape
    blocks = [value[:, i : i + LANES] for i in range(0, width, LANES)]
    left = blocks[-1].shape[1]
    if left < LANES:
        fold = rows * left // LANES
        blocks[-1] = jnp.concatenate(
            [blocks[-1][i : i + fold] for i in range(0, rows, fold)], axis=1
        )
    return jnp.concatenate(blocks, axis=0)


def unpacked(value, rows):
    whole, left = divmod(value.shape[0], rows)
    blocks = [value[i * rows : (i + 1) * rows] for i in range(whole)]
    if left:
        width = left * LANES // rows
        folded = value[whole * rows :]
        blocks.append(
            jnp.concatenate([folded[:, i : i + width] for i in range(0, LANES, width)], axis=0)
        )
    return jnp.concatenate(blocks, axis=1)


def fields_kernel(first, widths, has_total, last, *refs):
    refs = list(refs)
    core_ref = refs.pop(0)
    total_ref = refs.pop(0) if has_total else None
    high_ref, low_ref = refs[:2]
    outs = refs[-2:] if last else refs[-1:]
    total = None
    for place, piece in enumerate(refs[2 : -len(outs)], first):
        size = piece.shape[0]
        modes = slice(place * size, (place + 1) * size)
        high, low = halves(piece[...])
        product = dot(high_ref[:, modes], jnp.concatenate([high, low], axis=1))
        middle = product.shape[1] // 2
        product = product[:, :middle] + (product[:, middle:] + dot(low_ref[:, modes], high))
        total = product if total is None else total + product
    rows = total.shape[0] // 2
    real, imag = [], []
    start = 0
    for width in widths:
        middle, end = start + width, start + 2 * width
        real.append(total[:rows, start:middle] - total[rows:, middle:end])
        imag.append(total[:rows, middle:end] + total[rows:, start:middle])
        start = end
    real, imag = jnp.concatenate(real, axis=1), jnp.concatenate(imag, axis=1)
    if has_total:
        real, imag = real + total_ref[0], imag + total_ref[1]
    if last:
        first_core = core_ref[0] == 0
        real, imag = packed(real), packed(imag)
        outs[0][...] = jnp.where(first_core, real, imag)
        outs[1][...] = jnp.where(first_core, imag, real)
    else:
        outs[0][0], outs[0][1] = real, imag


def add_fields(matrix, pieces, first, widths, core, total=None, last=False):
    rows = matrix[0].shape[0] // 2
    size, width = pieces[0].shape[0], sum(widths)
    shape = packed_shape(rows, width) if last else (2, rows, width)
    out = jax.ShapeDtypeStruct(shape, jnp.float32)
    totals = [] if total is None else [total]
    count = len(pieces)
    return pl.pallas_call(
        functools.partial(fields_kernel, first, widths, total is not None, last),
        in_specs=[SMEM] + [VMEM] * (len(totals) + 2 + count),
        out_specs=[VMEM, VMEM] if last else VMEM,
        out_shape=[out, out] if last else out,
        compiler_params=params(12),
        cost_estimate=COST,
    )(core, *totals, *matrix, *pieces)


def residual(core_ref, kept_ref, other_ref, measured_ref, scale):
    first_core = core_ref[0] == 0
    rows = measured_ref.shape[0]
    kept, other = unpacked(kept_ref[...], rows), unpacked(other_ref[...], rows)
    real, imag = jnp.where(first_core, kept, other), jnp.where(first_core, other, kept)
    excess = real * real + imag * imag - measured_ref[...]
    real, imag = excess * real * scale, excess * imag * scale
    above, below = [], []
    for start, end in groups(0, real.shape[1]):
        above += [real[:, start:end], imag[:, start:end]]
        below += [imag[:, start:end], -real[:, start:end]]
    return jnp.concatenate(
        [jnp.concatenate(above, axis=1), jnp.concatenate(below, axis=1)], axis=0
    )


def gradient_tiles(chunks, scale, core_ref, refs):
    residuals = [residual(core_ref, *refs[3 * c : 3 * c + 3], scale) for c in range(chunks)]
    high, low = halves(jnp.concatenate(residuals, axis=1))
    left = jnp.concatenate([high, high, low], axis=1)
    for pieces in zip(*[iter(refs[3 * chunks :])] * chunks):
        high, low = halves(jnp.concatenate([piece[...] for piece in pieces], axis=1))
        product = dot(left, jnp.concatenate([high, low, high], axis=1), 1)
        yield product.reshape(2, product.shape[0] // 2, product.shape[1])


def part_kernel(chunks, scale, core_ref, *refs):
    out_ref = refs[-1]
    for place, product in enumerate(gradient_tiles(chunks, scale, core_ref, refs[:-1])):
        size = product.shape[2]
        out_ref[:, :, place * size : (place + 1) * size] = product


def last_kernel(chunks, scale, has_part, core_ref, order_ref, *refs):
    part_ref = refs[0] if has_part else None
    out_ref, slots_ref, done_ref = refs[-3:]
    copies = []
    for product in gradient_tiles(chunks, scale, core_ref, refs[has_part:-3]):
        slot, size = len(copies), product.shape[2]
        if has_part:
            product = product + part_ref[:, :, slot * size : (slot + 1) * size]
        slots_ref[slot] = product
        column = pl.multiple_of(order_ref[slot] * size, size)
        copies.append(
            pltpu.make_async_copy(
                slots_ref.at[slot], out_ref.at[:, :, pl.ds(column, size)], done_ref.at[slot]
            )
        )
        copies[-1].start()
    for copy in copies:
        copy.wait()


def add_gradient(core, order, sums, chunks, places, count, part=None, last=False):
    rows = sums[0][-1].shape[0]
    size, width = chunks[0][places[0]].shape[0], sum(measured.shape[1] for _, _, measured in sums)
    modes = len(places) * size
    operands = [value for chunk_sums in sums for value in chunk_sums]
    operands += [chunk[place] for place in places for chunk in chunks]
    options = dict(
        out_shape=jax.ShapeDtypeStruct((2, rows, modes), jnp.float32),
        cost_estimate=COST,
    )
    if not last:
        return pl.pallas_call(
            functools.partial(part_kernel, len(chunks), 1.0 / count),
            in_specs=[SMEM] + [VMEM] * len(operands),
            out_specs=VMEM,
            compiler_params=params(12),
            **options,
        )(core, *operands)
    if part is not None:
        operands.insert(0, part)
    return pl.pallas_call(
        functools.partial(last_kernel, len(chunks), 1.0 / count, part is not None),
        in_specs=[SMEM, SMEM] + [VMEM] * len(operands),
        out_specs=pl.BlockSpec(memory_space=pl.ANY),
        scratch_shapes=[
            pltpu.VMEM((len(places), 2, rows, size), jnp.float32),
            pltpu.SemaphoreType.DMA((len(places),)),
        ],
        compiler_params=params(20),
        **options,
    )(core, order, *operands)


def exchange(value, axis, size, mask):
    return lax.ppermute(value, axis, [(i, i ^ mask) for i in range(size)])


def mode_exchange(value, modes, mask):
    return exchange(value, "mode", modes, mask)


def square_body(row_size, mode_size, transfer_matrix, probes, intensity):
    half, count = probes.shape[1] // 2, probes.shape[2]
    row = lax.axis_index("row")
    core = (lax.axis_index("mode") % 2).astype(jnp.int32)[None]
    near = [(0, 0), (0, 1), (1, 0), (2, 1)]
    side = [(1, 1), (2, 0)]
    far = [(3, 0), (3, 1)]
    order = jnp.stack([(row ^ mask) * 2 + which for mask, which in near + side + far]).astype(jnp.int32)

    links = {
        1: [((0, 0), (1, 0)), ((0, 1), (1, 1)), ((2, 1), (3, 1))],
        2: [((0, 1), (2, 1)), ((0, 0), (2, 0)), ((1, 0), (3, 0))],
    }
    cut = count - 2 * LAST_PROBES
    spans = [(0, cut)] if cut else []
    spans += [(cut, cut + LAST_PROBES), (cut + LAST_PROBES, count)]
    ended = {1: [], 2: []}

    def send(chunk, step, *earlier):
        for mask, transfers in links.items():
            source, target = transfers[step]
            value = in_order(chunk[source], *ended[mask][-2:-1], *earlier)
            chunk[target] = exchange(value, "row", row_size, mask)
            ended[mask].append(chunk[target])

    def fields(chunk, places, first, **options):
        pieces = [chunk[place] for place in places]
        return add_fields(matrix, pieces, first, widths, core, **options)

    transfer_matrix = pltpu.with_memory_space_constraint(transfer_matrix, pltpu.HBM)
    probes = pltpu.with_memory_space_constraint(probes, pltpu.HBM)
    chunks = [dict(zip(near[:2], probe_chunk(probes, *span))) for span in spans]
    matrix = matrix_halves(transfer_matrix, order, half)
    places = near + side + far
    bits = [1 << bit for bit in range(1, mode_size.bit_length() - 1)]
    sums, waits = [], []
    part = None

    def tied(chunk, places, *earlier):
        for place in places:
            chunk[place] = in_order(chunk[place], *earlier)

    for c, (low, high) in enumerate(spans):
        chunk, widths = chunks[c], group_widths(low, high)
        last = c == len(spans) - 1
        send(chunk, 0, *waits)
        send(chunk, 1, *(sums[-1:] if c else []))
        if c:
            total = sums[-1]
            if not last:
                near_total = fields(chunk, near, 0)
                total = in_order(total, near_total)
            arrived = mode_exchange(total, mode_size, bits[0])
            if part is not None:
                arrived = in_order(arrived, part)
            total = total + arrived
            if last:
                tied(chunk, near[2:], total)
                near_total = fields(chunk, near, 0)
        else:
            near_total = fields(chunk, near, 0)
        send(chunk, 2, *([near_total] if c else matrix), *([] if part is None else [part]))
        if c:
            tied(chunk, side, total)
            if last:
                total = in_order(total, near_total)
                for mask in bits[1:]:
                    total = total + mode_exchange(total, mode_size, mask)
                tied(chunk, side, total)
        side_total = fields(chunk, side, len(near), total=near_total)
        if c:
            if not last:
                total = in_order(total, side_total)
                for mask in bits[1:]:
                    total = total + mode_exchange(total, mode_size, mask)
            tied(chunk, far, total)
            other = mode_exchange(total, mode_size, 1)
            if last:
                tied(chunk, far, other)
            sums[-1] = total, other, intensity[:, slice(*spans[c - 1])]
        if c == 1 and cut:
            part = add_gradient(core, order, sums, chunks[:1], places, count)
        kept, sent = fields(chunk, far, len(near + side), total=side_total, last=True)
        waits = [side_total, *(chunks[c + 1][place] for place in near[:2])] if not last else []
        sums.append(kept + mode_exchange(sent, mode_size, 1))
    arrived = [mode_exchange(sums[-1], mode_size, mask) for mask in range(2, mode_size, 2)]
    total = sum(arrived, sums[-1])
    sums[-1] = total, mode_exchange(total, mode_size, 1), intensity[:, slice(*spans[-1])]
    start = 1 if cut else 0
    return add_gradient(core, order, sums[start:], chunks[start:], places, count, part, True)


def plain_body(transfer_matrix, probes, intensity):
    dot = functools.partial(
        jnp.einsum, precision=lax.Precision.HIGHEST, preferred_element_type=jnp.float32
    )
    strip = lax.all_gather(probes, "row", axis=1, tiled=True)
    products = dot("amn,bnp->abmp", transfer_matrix, strip)
    fields = jnp.stack([products[0, 0] - products[1, 1], products[0, 1] + products[1, 0]])
    fields = lax.psum(fields, "mode")
    excess = fields[0] * fields[0] + fields[1] * fields[1] - intensity
    residual = excess[None] * fields / probes.shape[2]
    products = dot("amp,bnp->abmn", residual, strip)
    return jnp.stack([products[0, 0] + products[1, 1], products[1, 0] - products[0, 1]])


def solution(mesh):
    in_specs = (P(None, "row", "mode"), P(None, ("mode", "row"), None), P("row", None))
    out_specs = P(None, "row", "mode")
    row_size, mode_size = mesh.shape["row"], mesh.shape["mode"]

    def body(transfer_matrix, probes, intensity):
        square = (
            row_size == 4
            and mode_size & (mode_size - 1) == 0
            and mode_size > 1
            and probes.shape[1] % (2 * LANES) == 0
            and probes.shape[2] % LANES == 0
            and probes.shape[2] >= 2 * LAST_PROBES
            and transfer_matrix.shape[1] % 16 == 0
        )
        if square:
            return square_body(row_size, mode_size, transfer_matrix, probes, intensity)
        return plain_body(transfer_matrix, probes, intensity)

    return jax.shard_map(body, mesh=mesh, in_specs=in_specs, out_specs=out_specs, check_vma=False)
```

```python
import functools

import jax
import jax.numpy as jnp
from jax import lax
from jax.experimental import pallas as pl
from jax.experimental.pallas import tpu as pltpu
from jax.sharding import PartitionSpec as P

LANES = 128
LAST_PROBES = 64
MIB = 1024 * 1024
VMEM = pl.BlockSpec(memory_space=pltpu.VMEM)
SMEM = pl.BlockSpec(memory_space=pltpu.SMEM)
COST = pl.CostEstimate(flops=1000, bytes_accessed=1000, transcendentals=0)


def halves(value):
    high = value.astype(jnp.bfloat16)
    return high, (value - high.astype(jnp.float32)).astype(jnp.bfloat16)


def dot(left, right, dimension=0):
    return lax.dot_general(
        left, right, (((1,), (dimension,)), ((), ())), preferred_element_type=jnp.float32
    )


def params(mib):
    return pltpu.CompilerParams(vmem_limit_bytes=mib * MIB)


def in_order(value, *earlier):
    return lax.optimization_barrier((value, *earlier))[0]


def groups(low, high):
    cuts = [low, *range(low // LANES * LANES + LANES, high, LANES), high]
    return list(zip(cuts, cuts[1:]))


def group_widths(low, high):
    return [end - start for start, end in groups(low, high)]


def chunk_kernel(low, high, probes_ref, *refs):
    outs, (slots_ref, done_ref, slot_done_ref) = refs[:2], refs[2:]
    half = outs[0].shape[0]
    copies, later = [], []
    for which, out_ref in enumerate(outs):
        place = 0
        modes = pl.ds(which * half, half)
        for start, end in groups(low, high):
            block = pl.ds(start // LANES * LANES, LANES)
            for part in range(2):
                if end - start == LANES:
                    target = out_ref.at[:, pl.ds(place + part * LANES, LANES)]
                    copy = pltpu.make_async_copy(
                        probes_ref.at[part, modes, block], target, done_ref.at[len(copies)]
                    )
                    copies.append(copy)
                else:
                    slot = 2 * which + part
                    copy = pltpu.make_async_copy(
                        probes_ref.at[part, modes, block], slots_ref.at[slot], slot_done_ref.at[slot]
                    )
                    later.append((copy, out_ref, slot, place + part * (end - start), start, end))
                copy.start()
            place += 2 * (end - start)
    for copy, out_ref, slot, place, start, end in later:
        copy.wait()
        first = start % LANES
        out_ref[:, place : place + end - start] = slots_ref[slot, :, first : first + end - start]
    for copy in copies:
        copy.wait()


def probe_chunk(probes, low, high):
    half, width = probes.shape[1] // 2, high - low
    whole = sum(size == LANES for size in group_widths(low, high))
    return pl.pallas_call(
        functools.partial(chunk_kernel, low, high),
        in_specs=[pl.BlockSpec(memory_space=pl.ANY)],
        out_specs=[VMEM, VMEM],
        out_shape=[jax.ShapeDtypeStruct((half, 2 * width), jnp.float32)] * 2,
        scratch_shapes=[
            pltpu.VMEM((4, half, LANES), jnp.float32),
            pltpu.SemaphoreType.DMA((max(4 * whole, 1),)),
            pltpu.SemaphoreType.DMA((4,)),
        ],
        compiler_params=params(8),
        cost_estimate=COST,
    )(probes)


def matrix_kernel(order_ref, matrix_ref, high_ref, low_ref):
    high_ref[...], low_ref[...] = halves(matrix_ref[...].reshape(high_ref.shape))


def matrix_halves(matrix, order, half):
    _, rows, modes = matrix.shape
    out = jax.ShapeDtypeStruct((2 * rows, modes), jnp.bfloat16)
    spec = pl.BlockSpec((2 * rows, half), lambda i, _: (0, i))
    return pl.pallas_call(
        matrix_kernel,
        grid_spec=pltpu.PrefetchScalarGridSpec(
            num_scalar_prefetch=1,
            grid=(modes // half,),
            in_specs=[pl.BlockSpec((2, rows, half), lambda i, order_ref: (0, 0, order_ref[i]))],
            out_specs=[spec, spec],
        ),
        out_shape=[out, out],
        compiler_params=params(12),
        cost_estimate=COST,
    )(order, matrix)


def packed_shape(rows, width):
    return rows * width // LANES, LANES


def packed(value):
    rows, width = value.shape
    blocks = [value[:, i : i + LANES] for i in range(0, width, LANES)]
    left = blocks[-1].shape[1]
    if left < LANES:
        fold = rows * left // LANES
        blocks[-1] = jnp.concatenate(
            [blocks[-1][i : i + fold] for i in range(0, rows, fold)], axis=1
        )
    return jnp.concatenate(blocks, axis=0)


def unpacked(value, rows):
    whole, left = divmod(value.shape[0], rows)
    blocks = [value[i * rows : (i + 1) * rows] for i in range(whole)]
    if left:
        width = left * LANES // rows
        folded = value[whole * rows :]
        blocks.append(
            jnp.concatenate([folded[:, i : i + width] for i in range(0, LANES, width)], axis=0)
        )
    return jnp.concatenate(blocks, axis=1)


def fields_kernel(first, widths, has_total, last, *refs):
    refs = list(refs)
    core_ref = refs.pop(0)
    total_ref = refs.pop(0) if has_total else None
    high_ref, low_ref = refs[:2]
    outs = refs[-2:] if last else refs[-1:]
    total = None
    for place, piece in enumerate(refs[2 : -len(outs)], first):
        size = piece.shape[0]
        modes = slice(place * size, (place + 1) * size)
        high, low = halves(piece[...])
        product = dot(high_ref[:, modes], jnp.concatenate([high, low], axis=1))
        middle = product.shape[1] // 2
        product = product[:, :middle] + (product[:, middle:] + dot(low_ref[:, modes], high))
        total = product if total is None else total + product
    rows = total.shape[0] // 2
    real, imag = [], []
    start = 0
    for width in widths:
        middle, end = start + width, start + 2 * width
        real.append(total[:rows, start:middle] - total[rows:, middle:end])
        imag.append(total[:rows, middle:end] + total[rows:, start:middle])
        start = end
    real, imag = jnp.concatenate(real, axis=1), jnp.concatenate(imag, axis=1)
    if has_total:
        real, imag = real + total_ref[0], imag + total_ref[1]
    if last:
        first_core = core_ref[0] == 0
        real, imag = packed(real), packed(imag)
        outs[0][...] = jnp.where(first_core, real, imag)
        outs[1][...] = jnp.where(first_core, imag, real)
    else:
        outs[0][0], outs[0][1] = real, imag


def add_fields(matrix, pieces, first, widths, core, total=None, last=False):
    rows = matrix[0].shape[0] // 2
    size, width = pieces[0].shape[0], sum(widths)
    shape = packed_shape(rows, width) if last else (2, rows, width)
    out = jax.ShapeDtypeStruct(shape, jnp.float32)
    totals = [] if total is None else [total]
    count = len(pieces)
    return pl.pallas_call(
        functools.partial(fields_kernel, first, widths, total is not None, last),
        in_specs=[SMEM] + [VMEM] * (len(totals) + 2 + count),
        out_specs=[VMEM, VMEM] if last else VMEM,
        out_shape=[out, out] if last else out,
        compiler_params=params(12),
        cost_estimate=COST,
    )(core, *totals, *matrix, *pieces)


def residual(core_ref, kept_ref, other_ref, measured_ref, scale):
    first_core = core_ref[0] == 0
    rows = measured_ref.shape[0]
    kept, other = unpacked(kept_ref[...], rows), unpacked(other_ref[...], rows)
    real, imag = jnp.where(first_core, kept, other), jnp.where(first_core, other, kept)
    excess = real * real + imag * imag - measured_ref[...]
    real, imag = excess * real * scale, excess * imag * scale
    above, below = [], []
    for start, end in groups(0, real.shape[1]):
        above += [real[:, start:end], imag[:, start:end]]
        below += [imag[:, start:end], -real[:, start:end]]
    return jnp.concatenate(
        [jnp.concatenate(above, axis=1), jnp.concatenate(below, axis=1)], axis=0
    )


def gradient_tiles(scale, core_ref, sums, pieces):
    high, low = halves(residual(core_ref, *sums, scale))
    left = jnp.concatenate([high, high, low], axis=1)
    for place, piece in enumerate(pieces):
        high, low = halves(piece[...])
        product = dot(left, jnp.concatenate([high, low, high], axis=1), 1)
        size = product.shape[1]
        yield product.reshape(2, -1, size), slice(place * size, (place + 1) * size)


def part_kernel(scale, has_part, core_ref, *refs):
    out_ref = refs[-1]
    part_ref = refs[0] if has_part else None
    sums, pieces = refs[has_part : has_part + 3], refs[has_part + 3 : -1]
    for product, modes in gradient_tiles(scale, core_ref, sums, pieces):
        out_ref[:, :, modes] = product + part_ref[:, :, modes] if has_part else product


def gradient_part(core, sums, pieces, count, part=None):
    operands = [*sums, *pieces] if part is None else [part, *sums, *pieces]
    modes = len(pieces) * pieces[0].shape[0]
    return pl.pallas_call(
        functools.partial(part_kernel, 1.0 / count, part is not None),
        in_specs=[SMEM] + [VMEM] * len(operands),
        out_specs=VMEM,
        out_shape=jax.ShapeDtypeStruct((2, sums[-1].shape[0], modes), jnp.float32),
        input_output_aliases={} if part is None else {1: 0},
        compiler_params=params(12),
        cost_estimate=COST,
    )(core, *operands)


def last_kernel(scale, core_ref, order_ref, part_ref, *refs):
    pieces, (out_ref, slots_ref, done_ref) = refs[3:-3], refs[-3:]
    copies = []
    for product, modes in gradient_tiles(scale, core_ref, refs[:3], pieces):
        slot, size = len(copies), product.shape[2]
        slots_ref[slot] = product + part_ref[:, :, modes]
        column = pl.multiple_of(order_ref[slot] * size, size)
        copies.append(
            pltpu.make_async_copy(
                slots_ref.at[slot], out_ref.at[:, :, pl.ds(column, size)], done_ref.at[slot]
            )
        )
        copies[-1].start()
    for copy in copies:
        copy.wait()


def last_gradient(core, order, part, sums, pieces, count):
    operands = [part, *sums, *pieces]
    slots = (len(pieces), 2, part.shape[1], pieces[0].shape[0])
    return pl.pallas_call(
        functools.partial(last_kernel, 1.0 / count),
        in_specs=[SMEM, SMEM] + [VMEM] * len(operands),
        out_specs=pl.BlockSpec(memory_space=pl.ANY),
        out_shape=jax.ShapeDtypeStruct(part.shape, jnp.float32),
        scratch_shapes=[pltpu.VMEM(slots, jnp.float32), pltpu.SemaphoreType.DMA(slots[:1])],
        compiler_params=params(20),
        cost_estimate=COST,
    )(core, order, *operands)


def exchange(value, axis, size, mask):
    return lax.ppermute(value, axis, [(i, i ^ mask) for i in range(size)])


def mode_exchange(value, modes, mask):
    return exchange(value, "mode", modes, mask)


def square_body(row_size, mode_size, transfer_matrix, probes, intensity):
    half, count = probes.shape[1] // 2, probes.shape[2]
    row = lax.axis_index("row")
    core = (lax.axis_index("mode") % 2).astype(jnp.int32)[None]
    near = [(0, 0), (0, 1), (1, 0), (2, 1)]
    side = [(1, 1), (2, 0)]
    far = [(3, 0), (3, 1)]
    order = jnp.stack([(row ^ mask) * 2 + which for mask, which in near + side + far]).astype(jnp.int32)

    links = {
        1: [((0, 0), (1, 0)), ((0, 1), (1, 1)), ((2, 1), (3, 1))],
        2: [((0, 1), (2, 1)), ((0, 0), (2, 0)), ((1, 0), (3, 0))],
    }
    cut = count - 2 * LAST_PROBES
    spans = [(0, cut)] if cut else []
    spans += [(cut, cut + LAST_PROBES), (cut + LAST_PROBES, count)]
    ended = {1: [], 2: []}

    def send(chunk, step, *earlier):
        for mask, transfers in links.items():
            source, target = transfers[step]
            value = in_order(chunk[source], *ended[mask][-2:-1], *earlier)
            chunk[target] = exchange(value, "row", row_size, mask)
            ended[mask].append(chunk[target])

    def fields(chunk, places, first, **options):
        pieces = [chunk[place] for place in places]
        return add_fields(matrix, pieces, first, widths, core, **options)

    transfer_matrix = pltpu.with_memory_space_constraint(transfer_matrix, pltpu.HBM)
    probes = pltpu.with_memory_space_constraint(probes, pltpu.HBM)
    chunks = [dict(zip(near[:2], probe_chunk(probes, *span))) for span in spans]
    matrix = matrix_halves(transfer_matrix, order, half)
    places = near + side + far
    bits = [1 << bit for bit in range(1, mode_size.bit_length() - 1)]
    sums, waits = [], []
    part = None

    def tied(chunk, places, *earlier):
        for place in places:
            chunk[place] = in_order(chunk[place], *earlier)

    for c, (low, high) in enumerate(spans):
        chunk, widths = chunks[c], group_widths(low, high)
        last = c == len(spans) - 1
        send(chunk, 0, *waits)
        send(chunk, 1, *(sums[-1:] if c else []))
        if c:
            total = sums[-1]
            if not last:
                near_total = fields(chunk, near, 0)
                total = in_order(total, near_total)
            arrived = mode_exchange(total, mode_size, bits[0])
            if part is not None:
                arrived = in_order(arrived, part)
            total = total + arrived
            if last:
                tied(chunk, near[2:], total)
                near_total = fields(chunk, near, 0)
        else:
            near_total = fields(chunk, near, 0)
        send(chunk, 2, *([near_total] if c else matrix), *([] if part is None else [part]))
        if c:
            tied(chunk, side, total)
            if last:
                total = in_order(total, near_total)
                for mask in bits[1:]:
                    total = total + mode_exchange(total, mode_size, mask)
                tied(chunk, side, total)
        side_total = fields(chunk, side, len(near), total=near_total)
        if c:
            if not last:
                total = in_order(total, side_total)
                for mask in bits[1:]:
                    total = total + mode_exchange(total, mode_size, mask)
            tied(chunk, far, total)
            other = mode_exchange(total, mode_size, 1)
            if last:
                tied(chunk, far, other)
            sums[-1] = total, other, intensity[:, slice(*spans[c - 1])]
        if c == 1 and cut:
            part = gradient_part(core, sums[0], [chunks[0][place] for place in places], count)
        kept, sent = fields(chunk, far, len(near + side), total=side_total, last=True)
        waits = [side_total, *(chunks[c + 1][place] for place in near[:2])] if not last else []
        sums.append(kept + mode_exchange(sent, mode_size, 1))
    arrived = [mode_exchange(sums[-1], mode_size, mask) for mask in range(2, mode_size, 2)]
    pieces = [[chunk[place] for place in places] for chunk in chunks[-2:]]
    before = in_order(sums[-2][0], sums[-1]), *sums[-2][1:]
    part = gradient_part(core, before, pieces[0], count, part)
    total = sum((in_order(value, part) for value in arrived), sums[-1])
    sums[-1] = total, mode_exchange(total, mode_size, 1), intensity[:, slice(*spans[-1])]
    return last_gradient(core, order, part, sums[-1], pieces[1], count)


def plain_body(transfer_matrix, probes, intensity):
    dot = functools.partial(
        jnp.einsum, precision=lax.Precision.HIGHEST, preferred_element_type=jnp.float32
    )
    strip = lax.all_gather(probes, "row", axis=1, tiled=True)
    products = dot("amn,bnp->abmp", transfer_matrix, strip)
    fields = jnp.stack([products[0, 0] - products[1, 1], products[0, 1] + products[1, 0]])
    fields = lax.psum(fields, "mode")
    excess = fields[0] * fields[0] + fields[1] * fields[1] - intensity
    residual = excess[None] * fields / probes.shape[2]
    products = dot("amp,bnp->abmn", residual, strip)
    return jnp.stack([products[0, 0] + products[1, 1], products[1, 0] - products[0, 1]])


def solution(mesh):
    in_specs = (P(None, "row", "mode"), P(None, ("mode", "row"), None), P("row", None))
    out_specs = P(None, "row", "mode")
    row_size, mode_size = mesh.shape["row"], mesh.shape["mode"]

    def body(transfer_matrix, probes, intensity):
        square = (
            row_size == 4
            and mode_size & (mode_size - 1) == 0
            and mode_size > 1
            and probes.shape[1] % (2 * LANES) == 0
            and probes.shape[2] % LANES == 0
            and probes.shape[2] >= 2 * LAST_PROBES
            and transfer_matrix.shape[1] % 16 == 0
        )
        if square:
            return square_body(row_size, mode_size, transfer_matrix, probes, intensity)
        return plain_body(transfer_matrix, probes, intensity)

    return jax.shard_map(body, mesh=mesh, in_specs=in_specs, out_specs=out_specs, check_vma=False)
```

```python
import functools

import jax
import jax.numpy as jnp
from jax import lax
from jax.experimental import pallas as pl
from jax.experimental.pallas import tpu as pltpu
from jax.sharding import PartitionSpec as P

LANES = 128
LAST_PROBES = 64
MIB = 1024 * 1024
VMEM = pl.BlockSpec(memory_space=pltpu.VMEM)
SMEM = pl.BlockSpec(memory_space=pltpu.SMEM)
COST = pl.CostEstimate(flops=1000, bytes_accessed=1000, transcendentals=0)


def halves(value):
    high = value.astype(jnp.bfloat16)
    return high, (value - high.astype(jnp.float32)).astype(jnp.bfloat16)


def dot(left, right, dimension=0):
    return lax.dot_general(
        left, right, (((1,), (dimension,)), ((), ())), preferred_element_type=jnp.float32
    )


def params(mib):
    return pltpu.CompilerParams(vmem_limit_bytes=mib * MIB)


def in_order(value, *earlier):
    return lax.optimization_barrier((value, *earlier))[0]


def groups(low, high):
    cuts = [low, *range(low // LANES * LANES + LANES, high, LANES), high]
    return list(zip(cuts, cuts[1:]))


def group_widths(low, high):
    return [end - start for start, end in groups(low, high)]


def chunk_kernel(low, high, probes_ref, *refs):
    outs, (slots_ref, done_ref, slot_done_ref) = refs[:2], refs[2:]
    half = outs[0].shape[0]
    copies, later = [], []
    for which, out_ref in enumerate(outs):
        place = 0
        modes = pl.ds(which * half, half)
        for start, end in groups(low, high):
            block = pl.ds(start // LANES * LANES, LANES)
            for part in range(2):
                if end - start == LANES:
                    target = out_ref.at[:, pl.ds(place + part * LANES, LANES)]
                    copy = pltpu.make_async_copy(
                        probes_ref.at[part, modes, block], target, done_ref.at[len(copies)]
                    )
                    copies.append(copy)
                else:
                    slot = 2 * which + part
                    copy = pltpu.make_async_copy(
                        probes_ref.at[part, modes, block], slots_ref.at[slot], slot_done_ref.at[slot]
                    )
                    later.append((copy, out_ref, slot, place + part * (end - start), start, end))
                copy.start()
            place += 2 * (end - start)
    for copy, out_ref, slot, place, start, end in later:
        copy.wait()
        first = start % LANES
        out_ref[:, place : place + end - start] = slots_ref[slot, :, first : first + end - start]
    for copy in copies:
        copy.wait()


def probe_chunk(probes, low, high):
    half, width = probes.shape[1] // 2, high - low
    whole = sum(size == LANES for size in group_widths(low, high))
    return pl.pallas_call(
        functools.partial(chunk_kernel, low, high),
        in_specs=[pl.BlockSpec(memory_space=pl.ANY)],
        out_specs=[VMEM, VMEM],
        out_shape=[jax.ShapeDtypeStruct((half, 2 * width), jnp.float32)] * 2,
        scratch_shapes=[
            pltpu.VMEM((4, half, LANES), jnp.float32),
            pltpu.SemaphoreType.DMA((max(4 * whole, 1),)),
            pltpu.SemaphoreType.DMA((4,)),
        ],
        compiler_params=params(8),
        cost_estimate=COST,
    )(probes)


def matrix_kernel(order_ref, matrix_ref, high_ref, low_ref):
    high_ref[...], low_ref[...] = halves(matrix_ref[...].reshape(high_ref.shape))


def matrix_halves(matrix, order, half):
    _, rows, modes = matrix.shape
    out = jax.ShapeDtypeStruct((2 * rows, modes), jnp.bfloat16)
    spec = pl.BlockSpec((2 * rows, half), lambda i, _: (0, i))
    return pl.pallas_call(
        matrix_kernel,
        grid_spec=pltpu.PrefetchScalarGridSpec(
            num_scalar_prefetch=1,
            grid=(modes // half,),
            in_specs=[pl.BlockSpec((2, rows, half), lambda i, order_ref: (0, 0, order_ref[i]))],
            out_specs=[spec, spec],
        ),
        out_shape=[out, out],
        compiler_params=params(12),
        cost_estimate=COST,
    )(order, matrix)


def packed_shape(rows, width):
    return rows * width // LANES, LANES


def packed(value):
    rows, width = value.shape
    blocks = [value[:, i : i + LANES] for i in range(0, width, LANES)]
    left = blocks[-1].shape[1]
    if left < LANES:
        fold = rows * left // LANES
        blocks[-1] = jnp.concatenate(
            [blocks[-1][i : i + fold] for i in range(0, rows, fold)], axis=1
        )
    return jnp.concatenate(blocks, axis=0)


def unpacked(value, rows):
    whole, left = divmod(value.shape[0], rows)
    blocks = [value[i * rows : (i + 1) * rows] for i in range(whole)]
    if left:
        width = left * LANES // rows
        folded = value[whole * rows :]
        blocks.append(
            jnp.concatenate([folded[:, i : i + width] for i in range(0, LANES, width)], axis=0)
        )
    return jnp.concatenate(blocks, axis=1)


def fields_kernel(first, widths, has_total, last, *refs):
    refs = list(refs)
    core_ref = refs.pop(0)
    total_ref = refs.pop(0) if has_total else None
    high_ref, low_ref = refs[:2]
    outs = refs[-2:] if last else refs[-1:]
    total = None
    for place, piece in enumerate(refs[2 : -len(outs)], first):
        size = piece.shape[0]
        modes = slice(place * size, (place + 1) * size)
        high, low = halves(piece[...])
        product = dot(high_ref[:, modes], jnp.concatenate([high, low], axis=1))
        middle = product.shape[1] // 2
        product = product[:, :middle] + (product[:, middle:] + dot(low_ref[:, modes], high))
        total = product if total is None else total + product
    rows = total.shape[0] // 2
    real, imag = [], []
    start = 0
    for width in widths:
        middle, end = start + width, start + 2 * width
        real.append(total[:rows, start:middle] - total[rows:, middle:end])
        imag.append(total[:rows, middle:end] + total[rows:, start:middle])
        start = end
    real, imag = jnp.concatenate(real, axis=1), jnp.concatenate(imag, axis=1)
    if has_total:
        real, imag = real + total_ref[0], imag + total_ref[1]
    if last:
        first_core = core_ref[0] == 0
        real, imag = packed(real), packed(imag)
        outs[0][...] = jnp.where(first_core, real, imag)
        outs[1][...] = jnp.where(first_core, imag, real)
    else:
        outs[0][0], outs[0][1] = real, imag


def add_fields(matrix, pieces, first, widths, core, total=None, last=False):
    rows = matrix[0].shape[0] // 2
    size, width = pieces[0].shape[0], sum(widths)
    shape = packed_shape(rows, width) if last else (2, rows, width)
    out = jax.ShapeDtypeStruct(shape, jnp.float32)
    totals = [] if total is None else [total]
    count = len(pieces)
    return pl.pallas_call(
        functools.partial(fields_kernel, first, widths, total is not None, last),
        in_specs=[SMEM] + [VMEM] * (len(totals) + 2 + count),
        out_specs=[VMEM, VMEM] if last else VMEM,
        out_shape=[out, out] if last else out,
        compiler_params=params(12),
        cost_estimate=COST,
    )(core, *totals, *matrix, *pieces)


def residual(core_ref, kept_ref, other_ref, measured_ref, scale):
    first_core = core_ref[0] == 0
    rows = measured_ref.shape[0]
    kept, other = unpacked(kept_ref[...], rows), unpacked(other_ref[...], rows)
    real, imag = jnp.where(first_core, kept, other), jnp.where(first_core, other, kept)
    excess = real * real + imag * imag - measured_ref[...]
    real, imag = excess * real * scale, excess * imag * scale
    above, below = [], []
    for start, end in groups(0, real.shape[1]):
        above += [real[:, start:end], imag[:, start:end]]
        below += [imag[:, start:end], -real[:, start:end]]
    return jnp.concatenate(
        [jnp.concatenate(above, axis=1), jnp.concatenate(below, axis=1)], axis=0
    )


def gradient_tiles(scale, core_ref, sums, pieces):
    high, low = halves(residual(core_ref, *sums, scale))
    left = jnp.concatenate([high, high, low], axis=1)
    for place, piece in enumerate(pieces):
        high, low = halves(piece[...])
        product = dot(left, jnp.concatenate([high, low, high], axis=1), 1)
        size = product.shape[1]
        yield product.reshape(2, -1, size), slice(place * size, (place + 1) * size)


def part_kernel(scale, has_part, core_ref, *refs):
    out_ref = refs[-1]
    part_ref = refs[0] if has_part else None
    sums, pieces = refs[has_part : has_part + 3], refs[has_part + 3 : -1]
    for product, modes in gradient_tiles(scale, core_ref, sums, pieces):
        out_ref[:, :, modes] = product + part_ref[:, :, modes] if has_part else product


def gradient_part(core, sums, pieces, count, part=None):
    operands = [*sums, *pieces] if part is None else [part, *sums, *pieces]
    modes = len(pieces) * pieces[0].shape[0]
    return pl.pallas_call(
        functools.partial(part_kernel, 1.0 / count, part is not None),
        in_specs=[SMEM] + [VMEM] * len(operands),
        out_specs=VMEM,
        out_shape=jax.ShapeDtypeStruct((2, sums[-1].shape[0], modes), jnp.float32),
        input_output_aliases={} if part is None else {1: 0},
        compiler_params=params(12),
        cost_estimate=COST,
    )(core, *operands)


def last_kernel(scale, core_ref, order_ref, part_ref, *refs):
    pieces, (out_ref, slots_ref, done_ref) = refs[3:-3], refs[-3:]
    copies = []
    for product, modes in gradient_tiles(scale, core_ref, refs[:3], pieces):
        slot, size = len(copies), product.shape[2]
        slots_ref[slot] = product + part_ref[:, :, modes]
        column = pl.multiple_of(order_ref[slot] * size, size)
        copies.append(
            pltpu.make_async_copy(
                slots_ref.at[slot], out_ref.at[:, :, pl.ds(column, size)], done_ref.at[slot]
            )
        )
        copies[-1].start()
    for copy in copies:
        copy.wait()


def last_gradient(core, order, part, sums, pieces, count):
    operands = [part, *sums, *pieces]
    slots = (len(pieces), 2, part.shape[1], pieces[0].shape[0])
    return pl.pallas_call(
        functools.partial(last_kernel, 1.0 / count),
        in_specs=[SMEM, SMEM] + [VMEM] * len(operands),
        out_specs=pl.BlockSpec(memory_space=pl.ANY),
        out_shape=jax.ShapeDtypeStruct(part.shape, jnp.float32),
        scratch_shapes=[pltpu.VMEM(slots, jnp.float32), pltpu.SemaphoreType.DMA(slots[:1])],
        compiler_params=params(20),
        cost_estimate=COST,
    )(core, order, *operands)


def exchange(value, axis, size, mask):
    return lax.ppermute(value, axis, [(i, i ^ mask) for i in range(size)])


def mode_exchange(value, modes, mask):
    return exchange(value, "mode", modes, mask)


def square_body(row_size, mode_size, transfer_matrix, probes, intensity):
    half, count = probes.shape[1] // 2, probes.shape[2]
    row = lax.axis_index("row")
    core = (lax.axis_index("mode") % 2).astype(jnp.int32)[None]
    near = [(0, 0), (0, 1), (1, 0), (2, 1)]
    side = [(1, 1), (2, 0)]
    far = [(3, 0), (3, 1)]
    order = jnp.stack([(row ^ mask) * 2 + which for mask, which in near + side + far]).astype(jnp.int32)

    links = {
        1: [((0, 0), (1, 0)), ((0, 1), (1, 1)), ((2, 1), (3, 1))],
        2: [((0, 1), (2, 1)), ((0, 0), (2, 0)), ((1, 0), (3, 0))],
    }
    cut = count - 2 * LAST_PROBES
    spans = [(0, cut)] if cut else []
    spans += [(cut, cut + LAST_PROBES), (cut + LAST_PROBES, count)]
    ended = {1: [], 2: []}

    def send(chunk, step, *earlier):
        for mask, transfers in links.items():
            source, target = transfers[step]
            value = in_order(chunk[source], *ended[mask][-2:-1], *earlier)
            chunk[target] = exchange(value, "row", row_size, mask)
            ended[mask].append(chunk[target])

    def fields(chunk, places, first, **options):
        pieces = [chunk[place] for place in places]
        return add_fields(matrix, pieces, first, widths, core, **options)

    transfer_matrix = pltpu.with_memory_space_constraint(transfer_matrix, pltpu.HBM)
    probes = pltpu.with_memory_space_constraint(probes, pltpu.HBM)
    chunks = [dict(zip(near[:2], probe_chunk(probes, *span))) for span in spans]
    matrix = matrix_halves(transfer_matrix, order, half)
    places = near + side + far
    bits = [1 << bit for bit in range(1, mode_size.bit_length() - 1)]
    sums, waits = [], []
    part = None

    def tied(chunk, places, *earlier):
        for place in places:
            chunk[place] = in_order(chunk[place], *earlier)

    for c, (low, high) in enumerate(spans):
        chunk, widths = chunks[c], group_widths(low, high)
        last = c == len(spans) - 1
        send(chunk, 0, *waits)
        send(chunk, 1, *(sums[-1:] if c else []))
        if c:
            total = sums[-1]
            if not last:
                near_total = fields(chunk, near, 0)
                total = in_order(total, near_total)
            total = total + mode_exchange(total, mode_size, bits[0])
            if last:
                tied(chunk, near[2:], total)
                near_total = fields(chunk, near, 0)
        else:
            near_total = fields(chunk, near, 0)
        send(chunk, 2, *([] if last else [near_total] if c else matrix))
        if c:
            tied(chunk, side, total)
            if last:
                if cut:
                    before = in_order(sums[0][0], near_total), *sums[0][1:]
                    part = gradient_part(core, before, [chunks[0][place] for place in places], count)
                total = in_order(total, near_total)
                for mask in bits[1:]:
                    arrived = mode_exchange(total, mode_size, mask)
                    total = total + (in_order(arrived, part) if cut else arrived)
                tied(chunk, side, total)
        side_total = fields(chunk, side, len(near), total=near_total)
        if c:
            if not last:
                total = in_order(total, side_total)
                for mask in bits[1:]:
                    total = total + mode_exchange(total, mode_size, mask)
            tied(chunk, far, total)
            other = mode_exchange(total, mode_size, 1)
            if last:
                tied(chunk, far, other)
            sums[-1] = total, other, intensity[:, slice(*spans[c - 1])]
        kept, sent = fields(chunk, far, len(near + side), total=side_total, last=True)
        waits = [side_total, *(chunks[c + 1][place] for place in near[:2])] if not last else []
        sums.append(kept + mode_exchange(sent, mode_size, 1))
    arrived = [mode_exchange(sums[-1], mode_size, mask) for mask in range(2, mode_size, 2)]
    pieces = [[chunk[place] for place in places] for chunk in chunks[-2:]]
    before = in_order(sums[-2][0], sums[-1]), *sums[-2][1:]
    part = gradient_part(core, before, pieces[0], count, part)
    total = sum((in_order(value, part) for value in arrived), sums[-1])
    sums[-1] = total, mode_exchange(total, mode_size, 1), intensity[:, slice(*spans[-1])]
    return last_gradient(core, order, part, sums[-1], pieces[1], count)


def plain_body(transfer_matrix, probes, intensity):
    dot = functools.partial(
        jnp.einsum, precision=lax.Precision.HIGHEST, preferred_element_type=jnp.float32
    )
    strip = lax.all_gather(probes, "row", axis=1, tiled=True)
    products = dot("amn,bnp->abmp", transfer_matrix, strip)
    fields = jnp.stack([products[0, 0] - products[1, 1], products[0, 1] + products[1, 0]])
    fields = lax.psum(fields, "mode")
    excess = fields[0] * fields[0] + fields[1] * fields[1] - intensity
    residual = excess[None] * fields / probes.shape[2]
    products = dot("amp,bnp->abmn", residual, strip)
    return jnp.stack([products[0, 0] + products[1, 1], products[1, 0] - products[0, 1]])


def solution(mesh):
    in_specs = (P(None, "row", "mode"), P(None, ("mode", "row"), None), P("row", None))
    out_specs = P(None, "row", "mode")
    row_size, mode_size = mesh.shape["row"], mesh.shape["mode"]

    def body(transfer_matrix, probes, intensity):
        square = (
            row_size == 4
            and mode_size & (mode_size - 1) == 0
            and mode_size > 1
            and probes.shape[1] % (2 * LANES) == 0
            and probes.shape[2] % LANES == 0
            and probes.shape[2] >= 2 * LAST_PROBES
            and transfer_matrix.shape[1] % 16 == 0
        )
        if square:
            return square_body(row_size, mode_size, transfer_matrix, probes, intensity)
        return plain_body(transfer_matrix, probes, intensity)

    return jax.shard_map(body, mesh=mesh, in_specs=in_specs, out_specs=out_specs, check_vma=False)
```

```python
import functools

import jax
import jax.numpy as jnp
from jax import lax
from jax.experimental import pallas as pl
from jax.experimental.pallas import tpu as pltpu
from jax.sharding import PartitionSpec as P

LANES = 128
LAST_PROBES = 64
MIB = 1024 * 1024
VMEM = pl.BlockSpec(memory_space=pltpu.VMEM)
SMEM = pl.BlockSpec(memory_space=pltpu.SMEM)
COST = pl.CostEstimate(flops=1000, bytes_accessed=1000, transcendentals=0)


def halves(value):
    high = value.astype(jnp.bfloat16)
    return high, (value - high.astype(jnp.float32)).astype(jnp.bfloat16)


def dot(left, right, dimension=0):
    return lax.dot_general(
        left, right, (((1,), (dimension,)), ((), ())), preferred_element_type=jnp.float32
    )


def params(mib):
    return pltpu.CompilerParams(vmem_limit_bytes=mib * MIB)


def in_order(value, *earlier):
    return lax.optimization_barrier((value, *earlier))[0]


def groups(low, high):
    cuts = [low, *range(low // LANES * LANES + LANES, high, LANES), high]
    return list(zip(cuts, cuts[1:]))


def group_widths(low, high):
    return [end - start for start, end in groups(low, high)]


def chunk_kernel(low, high, probes_ref, *refs):
    outs, (slots_ref, done_ref, slot_done_ref) = refs[:2], refs[2:]
    half = outs[0].shape[0]
    copies, later = [], []
    for which, out_ref in enumerate(outs):
        place = 0
        modes = pl.ds(which * half, half)
        for start, end in groups(low, high):
            block = pl.ds(start // LANES * LANES, LANES)
            for part in range(2):
                if end - start == LANES:
                    target = out_ref.at[:, pl.ds(place + part * LANES, LANES)]
                    copy = pltpu.make_async_copy(
                        probes_ref.at[part, modes, block], target, done_ref.at[len(copies)]
                    )
                    copies.append(copy)
                else:
                    slot = 2 * which + part
                    copy = pltpu.make_async_copy(
                        probes_ref.at[part, modes, block], slots_ref.at[slot], slot_done_ref.at[slot]
                    )
                    later.append((copy, out_ref, slot, place + part * (end - start), start, end))
                copy.start()
            place += 2 * (end - start)
    for copy, out_ref, slot, place, start, end in later:
        copy.wait()
        first = start % LANES
        out_ref[:, place : place + end - start] = slots_ref[slot, :, first : first + end - start]
    for copy in copies:
        copy.wait()


def probe_chunk(probes, low, high):
    half, width = probes.shape[1] // 2, high - low
    whole = sum(size == LANES for size in group_widths(low, high))
    return pl.pallas_call(
        functools.partial(chunk_kernel, low, high),
        in_specs=[pl.BlockSpec(memory_space=pl.ANY)],
        out_specs=[VMEM, VMEM],
        out_shape=[jax.ShapeDtypeStruct((half, 2 * width), jnp.float32)] * 2,
        scratch_shapes=[
            pltpu.VMEM((4, half, LANES), jnp.float32),
            pltpu.SemaphoreType.DMA((max(4 * whole, 1),)),
            pltpu.SemaphoreType.DMA((4,)),
        ],
        compiler_params=params(8),
        cost_estimate=COST,
    )(probes)


def matrix_kernel(order_ref, matrix_ref, high_ref, low_ref):
    high_ref[...], low_ref[...] = halves(matrix_ref[...].reshape(high_ref.shape))


def matrix_halves(matrix, order, half):
    _, rows, modes = matrix.shape
    out = jax.ShapeDtypeStruct((2 * rows, modes), jnp.bfloat16)
    spec = pl.BlockSpec((2 * rows, half), lambda i, _: (0, i))
    return pl.pallas_call(
        matrix_kernel,
        grid_spec=pltpu.PrefetchScalarGridSpec(
            num_scalar_prefetch=1,
            grid=(modes // half,),
            in_specs=[pl.BlockSpec((2, rows, half), lambda i, order_ref: (0, 0, order_ref[i]))],
            out_specs=[spec, spec],
        ),
        out_shape=[out, out],
        compiler_params=params(12),
        cost_estimate=COST,
    )(order, matrix)


def packed_shape(rows, width):
    return rows * width // LANES, LANES


def packed(value):
    rows, width = value.shape
    blocks = [value[:, i : i + LANES] for i in range(0, width, LANES)]
    left = blocks[-1].shape[1]
    if left < LANES:
        fold = rows * left // LANES
        blocks[-1] = jnp.concatenate(
            [blocks[-1][i : i + fold] for i in range(0, rows, fold)], axis=1
        )
    return jnp.concatenate(blocks, axis=0)


def unpacked(value, rows):
    whole, left = divmod(value.shape[0], rows)
    blocks = [value[i * rows : (i + 1) * rows] for i in range(whole)]
    if left:
        width = left * LANES // rows
        folded = value[whole * rows :]
        blocks.append(
            jnp.concatenate([folded[:, i : i + width] for i in range(0, LANES, width)], axis=0)
        )
    return jnp.concatenate(blocks, axis=1)


def fields_kernel(first, widths, has_total, last, *refs):
    refs = list(refs)
    core_ref = refs.pop(0)
    total_ref = refs.pop(0) if has_total else None
    high_ref, low_ref = refs[:2]
    outs = refs[-2:] if last else refs[-1:]
    total = None
    for place, piece in enumerate(refs[2 : -len(outs)], first):
        size = piece.shape[0]
        modes = slice(place * size, (place + 1) * size)
        high, low = halves(piece[...])
        product = dot(high_ref[:, modes], jnp.concatenate([high, low], axis=1))
        middle = product.shape[1] // 2
        product = product[:, :middle] + (product[:, middle:] + dot(low_ref[:, modes], high))
        total = product if total is None else total + product
    rows = total.shape[0] // 2
    real, imag = [], []
    start = 0
    for width in widths:
        middle, end = start + width, start + 2 * width
        real.append(total[:rows, start:middle] - total[rows:, middle:end])
        imag.append(total[:rows, middle:end] + total[rows:, start:middle])
        start = end
    real, imag = jnp.concatenate(real, axis=1), jnp.concatenate(imag, axis=1)
    if has_total:
        real, imag = real + total_ref[0], imag + total_ref[1]
    if last:
        first_core = core_ref[0] == 0
        real, imag = packed(real), packed(imag)
        outs[0][...] = jnp.where(first_core, real, imag)
        outs[1][...] = jnp.where(first_core, imag, real)
    else:
        outs[0][0], outs[0][1] = real, imag


def add_fields(matrix, pieces, first, widths, core, total=None, last=False):
    rows = matrix[0].shape[0] // 2
    size, width = pieces[0].shape[0], sum(widths)
    shape = packed_shape(rows, width) if last else (2, rows, width)
    out = jax.ShapeDtypeStruct(shape, jnp.float32)
    totals = [] if total is None else [total]
    count = len(pieces)
    return pl.pallas_call(
        functools.partial(fields_kernel, first, widths, total is not None, last),
        in_specs=[SMEM] + [VMEM] * (len(totals) + 2 + count),
        out_specs=[VMEM, VMEM] if last else VMEM,
        out_shape=[out, out] if last else out,
        compiler_params=params(12),
        cost_estimate=COST,
    )(core, *totals, *matrix, *pieces)


def residual(core_ref, kept_ref, other_ref, measured_ref, scale):
    first_core = core_ref[0] == 0
    rows = measured_ref.shape[0]
    kept, other = unpacked(kept_ref[...], rows), unpacked(other_ref[...], rows)
    real, imag = jnp.where(first_core, kept, other), jnp.where(first_core, other, kept)
    excess = real * real + imag * imag - measured_ref[...]
    real, imag = excess * real * scale, excess * imag * scale
    above, below = [], []
    for start, end in groups(0, real.shape[1]):
        above += [real[:, start:end], imag[:, start:end]]
        below += [imag[:, start:end], -real[:, start:end]]
    return jnp.concatenate(
        [jnp.concatenate(above, axis=1), jnp.concatenate(below, axis=1)], axis=0
    )


def gradient_tiles(scale, core_ref, sums, pieces):
    high, low = halves(residual(core_ref, *sums, scale))
    left = jnp.concatenate([high, high, low], axis=1)
    for place, piece in enumerate(pieces):
        high, low = halves(piece[...])
        product = dot(left, jnp.concatenate([high, low, high], axis=1), 1)
        size = product.shape[1]
        yield product.reshape(2, -1, size), slice(place * size, (place + 1) * size)


def part_kernel(scale, parts, core_ref, *refs):
    out_ref = refs[-1]
    sums, pieces = refs[parts : parts + 3], refs[parts + 3 : -1]
    tiles = [
        part_ref.at[:, :, pl.ds(first, pieces[0].shape[0])]
        for part_ref in refs[:parts]
        for first in range(0, part_ref.shape[2], pieces[0].shape[0])
    ]
    for place, (product, modes) in enumerate(gradient_tiles(scale, core_ref, sums, pieces)):
        out_ref[:, :, modes] = product + tiles[place][...] if parts else product


def gradient_part(core, sums, pieces, count, parts=()):
    operands = [*parts, *sums, *pieces]
    modes = len(pieces) * pieces[0].shape[0]
    return pl.pallas_call(
        functools.partial(part_kernel, 1.0 / count, len(parts)),
        in_specs=[SMEM] + [VMEM] * len(operands),
        out_specs=VMEM,
        out_shape=jax.ShapeDtypeStruct((2, sums[-1].shape[0], modes), jnp.float32),
        compiler_params=params(12),
        cost_estimate=COST,
    )(core, *operands)


def last_kernel(scale, core_ref, order_ref, part_ref, *refs):
    pieces, (out_ref, slots_ref, done_ref) = refs[3:-3], refs[-3:]
    copies = []
    for product, modes in gradient_tiles(scale, core_ref, refs[:3], pieces):
        slot, size = len(copies), product.shape[2]
        slots_ref[slot] = product + part_ref[:, :, modes]
        column = pl.multiple_of(order_ref[slot] * size, size)
        copies.append(
            pltpu.make_async_copy(
                slots_ref.at[slot], out_ref.at[:, :, pl.ds(column, size)], done_ref.at[slot]
            )
        )
        copies[-1].start()
    for copy in copies:
        copy.wait()


def last_gradient(core, order, part, sums, pieces, count):
    operands = [part, *sums, *pieces]
    slots = (len(pieces), 2, part.shape[1], pieces[0].shape[0])
    return pl.pallas_call(
        functools.partial(last_kernel, 1.0 / count),
        in_specs=[SMEM, SMEM] + [VMEM] * len(operands),
        out_specs=pl.BlockSpec(memory_space=pl.ANY),
        out_shape=jax.ShapeDtypeStruct(part.shape, jnp.float32),
        scratch_shapes=[pltpu.VMEM(slots, jnp.float32), pltpu.SemaphoreType.DMA(slots[:1])],
        compiler_params=params(20),
        cost_estimate=COST,
    )(core, order, *operands)


def exchange(value, axis, size, mask):
    return lax.ppermute(value, axis, [(i, i ^ mask) for i in range(size)])


def mode_exchange(value, modes, mask):
    return exchange(value, "mode", modes, mask)


def square_body(row_size, mode_size, transfer_matrix, probes, intensity):
    half, count = probes.shape[1] // 2, probes.shape[2]
    row = lax.axis_index("row")
    core = (lax.axis_index("mode") % 2).astype(jnp.int32)[None]
    near = [(0, 0), (0, 1), (1, 0), (2, 1)]
    side = [(1, 1), (2, 0)]
    far = [(3, 0), (3, 1)]
    order = jnp.stack([(row ^ mask) * 2 + which for mask, which in near + side + far]).astype(jnp.int32)

    links = {
        1: [((0, 0), (1, 0)), ((0, 1), (1, 1)), ((2, 1), (3, 1))],
        2: [((0, 1), (2, 1)), ((0, 0), (2, 0)), ((1, 0), (3, 0))],
    }
    cut = count - 2 * LAST_PROBES
    spans = [(0, cut)] if cut else []
    spans += [(cut, cut + LAST_PROBES), (cut + LAST_PROBES, count)]
    ended = {1: [], 2: []}

    def send(chunk, step, *earlier):
        for mask, transfers in links.items():
            source, target = transfers[step]
            value = in_order(chunk[source], *ended[mask][-2:-1], *earlier)
            chunk[target] = exchange(value, "row", row_size, mask)
            ended[mask].append(chunk[target])

    def fields(chunk, places, first, **options):
        pieces = [chunk[place] for place in places]
        return add_fields(matrix, pieces, first, widths, core, **options)

    transfer_matrix = pltpu.with_memory_space_constraint(transfer_matrix, pltpu.HBM)
    probes = pltpu.with_memory_space_constraint(probes, pltpu.HBM)
    chunks = [dict(zip(near[:2], probe_chunk(probes, *span))) for span in spans]
    matrix = matrix_halves(transfer_matrix, order, half)
    places = near + side + far
    bits = [1 << bit for bit in range(1, mode_size.bit_length() - 1)]
    sums, waits, parts = [], [], []

    def tied(chunk, places, *earlier):
        for place in places:
            chunk[place] = in_order(chunk[place], *earlier)

    def first_part(places, *earlier):
        if cut:
            before = in_order(sums[0][0], *earlier), *sums[0][1:]
            pieces = [chunks[0][place] for place in places]
            parts.append(gradient_part(core, before, pieces, count))

    for c, (low, high) in enumerate(spans):
        chunk, widths = chunks[c], group_widths(low, high)
        last = c == len(spans) - 1
        send(chunk, 0, *waits)
        send(chunk, 1, *(sums[-1:] if c else []))
        if last:
            first_part(near, sums[-1])
            total = in_order(sums[-1], *(chunk[place] for place in near[2:]), *parts)
            arrived = mode_exchange(total, mode_size, bits[0])
            near_total = fields(chunk, near, 0)
            total = total + in_order(arrived, near_total)
            send(chunk, 2, *parts)
            first_part(side + far, near_total)
            for mask in bits[1:]:
                total = total + in_order(mode_exchange(total, mode_size, mask), *parts)
            tied(chunk, side, total)
            side_total = fields(chunk, side, len(near), total=near_total)
        else:
            near_total = fields(chunk, near, 0)
            if c:
                total = in_order(sums[-1], near_total)
                total = total + mode_exchange(total, mode_size, bits[0])
                tied(chunk, side, total)
            send(chunk, 2, *([near_total] if c else matrix))
            side_total = fields(chunk, side, len(near), total=near_total)
            if c:
                total = in_order(total, side_total)
                for mask in bits[1:]:
                    total = total + mode_exchange(total, mode_size, mask)
        if c:
            other = mode_exchange(total, mode_size, 1)
            tied(chunk, far, total, *([other] if last else []))
            sums[-1] = total, other, intensity[:, slice(*spans[c - 1])]
        kept, sent = fields(chunk, far, len(near + side), total=side_total, last=True)
        waits = [side_total, *(chunks[c + 1][place] for place in near[:2])] if not last else []
        sums.append(kept + mode_exchange(sent, mode_size, 1))
    arrived = [mode_exchange(sums[-1], mode_size, mask) for mask in (2, *range(mode_size - 2, 2, -2))]
    pieces = [[chunk[place] for place in places] for chunk in chunks[-2:]]
    before = in_order(sums[-2][0], sums[-1]), *sums[-2][1:]
    part = gradient_part(core, before, pieces[0], count, parts)
    total = sum((in_order(value, part) for value in arrived), sums[-1])
    sums[-1] = total, mode_exchange(total, mode_size, 1), intensity[:, slice(*spans[-1])]
    return last_gradient(core, order, part, sums[-1], pieces[1], count)


def plain_body(transfer_matrix, probes, intensity):
    dot = functools.partial(
        jnp.einsum, precision=lax.Precision.HIGHEST, preferred_element_type=jnp.float32
    )
    strip = lax.all_gather(probes, "row", axis=1, tiled=True)
    products = dot("amn,bnp->abmp", transfer_matrix, strip)
    fields = jnp.stack([products[0, 0] - products[1, 1], products[0, 1] + products[1, 0]])
    fields = lax.psum(fields, "mode")
    excess = fields[0] * fields[0] + fields[1] * fields[1] - intensity
    residual = excess[None] * fields / probes.shape[2]
    products = dot("amp,bnp->abmn", residual, strip)
    return jnp.stack([products[0, 0] + products[1, 1], products[1, 0] - products[0, 1]])


def solution(mesh):
    in_specs = (P(None, "row", "mode"), P(None, ("mode", "row"), None), P("row", None))
    out_specs = P(None, "row", "mode")
    row_size, mode_size = mesh.shape["row"], mesh.shape["mode"]

    def body(transfer_matrix, probes, intensity):
        square = (
            row_size == 4
            and mode_size & (mode_size - 1) == 0
            and mode_size > 1
            and probes.shape[1] % (2 * LANES) == 0
            and probes.shape[2] % LANES == 0
            and probes.shape[2] >= 2 * LAST_PROBES
            and transfer_matrix.shape[1] % 16 == 0
        )
        if square:
            return square_body(row_size, mode_size, transfer_matrix, probes, intensity)
        return plain_body(transfer_matrix, probes, intensity)

    return jax.shard_map(body, mesh=mesh, in_specs=in_specs, out_specs=out_specs, check_vma=False)
```

```python
import functools

import jax
import jax.numpy as jnp
from jax import lax
from jax.experimental import pallas as pl
from jax.experimental.pallas import tpu as pltpu
from jax.sharding import PartitionSpec as P

LANES = 128
LAST_PROBES = 64
MIB = 1024 * 1024
VMEM = pl.BlockSpec(memory_space=pltpu.VMEM)
SMEM = pl.BlockSpec(memory_space=pltpu.SMEM)
COST = pl.CostEstimate(flops=1000, bytes_accessed=1000, transcendentals=0)


def halves(value):
    high = value.astype(jnp.bfloat16)
    return high, (value - high.astype(jnp.float32)).astype(jnp.bfloat16)


def dot(left, right, dimension=0):
    return lax.dot_general(
        left, right, (((1,), (dimension,)), ((), ())), preferred_element_type=jnp.float32
    )


def params(mib):
    return pltpu.CompilerParams(vmem_limit_bytes=mib * MIB)


def in_order(value, *earlier):
    return lax.optimization_barrier((value, *earlier))[0]


def groups(low, high):
    cuts = [low, *range(low // LANES * LANES + LANES, high, LANES), high]
    return list(zip(cuts, cuts[1:]))


def group_widths(low, high):
    return [end - start for start, end in groups(low, high)]


def chunk_kernel(low, high, probes_ref, *refs):
    outs, (slots_ref, done_ref, slot_done_ref) = refs[:2], refs[2:]
    half = outs[0].shape[0]
    copies, later = [], []
    for which, out_ref in enumerate(outs):
        place = 0
        modes = pl.ds(which * half, half)
        for start, end in groups(low, high):
            block = pl.ds(start // LANES * LANES, LANES)
            for part in range(2):
                if end - start == LANES:
                    target = out_ref.at[:, pl.ds(place + part * LANES, LANES)]
                    copy = pltpu.make_async_copy(
                        probes_ref.at[part, modes, block], target, done_ref.at[len(copies)]
                    )
                    copies.append(copy)
                else:
                    slot = 2 * which + part
                    copy = pltpu.make_async_copy(
                        probes_ref.at[part, modes, block], slots_ref.at[slot], slot_done_ref.at[slot]
                    )
                    later.append((copy, out_ref, slot, place + part * (end - start), start, end))
                copy.start()
            place += 2 * (end - start)
    for copy, out_ref, slot, place, start, end in later:
        copy.wait()
        first = start % LANES
        out_ref[:, place : place + end - start] = slots_ref[slot, :, first : first + end - start]
    for copy in copies:
        copy.wait()


def probe_chunk(probes, low, high):
    half, width = probes.shape[1] // 2, high - low
    whole = sum(size == LANES for size in group_widths(low, high))
    return pl.pallas_call(
        functools.partial(chunk_kernel, low, high),
        in_specs=[pl.BlockSpec(memory_space=pl.ANY)],
        out_specs=[VMEM, VMEM],
        out_shape=[jax.ShapeDtypeStruct((half, 2 * width), jnp.float32)] * 2,
        scratch_shapes=[
            pltpu.VMEM((4, half, LANES), jnp.float32),
            pltpu.SemaphoreType.DMA((max(4 * whole, 1),)),
            pltpu.SemaphoreType.DMA((4,)),
        ],
        compiler_params=params(8),
        cost_estimate=COST,
    )(probes)


def matrix_kernel(order_ref, matrix_ref, high_ref, low_ref):
    high_ref[...], low_ref[...] = halves(matrix_ref[...].reshape(high_ref.shape))


def matrix_halves(matrix, order, half):
    _, rows, modes = matrix.shape
    out = jax.ShapeDtypeStruct((2 * rows, modes), jnp.bfloat16)
    spec = pl.BlockSpec((2 * rows, half), lambda i, _: (0, i))
    return pl.pallas_call(
        matrix_kernel,
        grid_spec=pltpu.PrefetchScalarGridSpec(
            num_scalar_prefetch=1,
            grid=(modes // half,),
            in_specs=[pl.BlockSpec((2, rows, half), lambda i, order_ref: (0, 0, order_ref[i]))],
            out_specs=[spec, spec],
        ),
        out_shape=[out, out],
        compiler_params=params(12),
        cost_estimate=COST,
    )(order, matrix)


def packed_shape(rows, width):
    return rows * width // LANES, LANES


def packed(value):
    rows, width = value.shape
    blocks = [value[:, i : i + LANES] for i in range(0, width, LANES)]
    left = blocks[-1].shape[1]
    if left < LANES:
        fold = rows * left // LANES
        blocks[-1] = jnp.concatenate(
            [blocks[-1][i : i + fold] for i in range(0, rows, fold)], axis=1
        )
    return jnp.concatenate(blocks, axis=0)


def unpacked(value, rows):
    whole, left = divmod(value.shape[0], rows)
    blocks = [value[i * rows : (i + 1) * rows] for i in range(whole)]
    if left:
        width = left * LANES // rows
        folded = value[whole * rows :]
        blocks.append(
            jnp.concatenate([folded[:, i : i + width] for i in range(0, LANES, width)], axis=0)
        )
    return jnp.concatenate(blocks, axis=1)


def fields_kernel(first, widths, has_total, last, *refs):
    refs = list(refs)
    core_ref = refs.pop(0)
    total_ref = refs.pop(0) if has_total else None
    high_ref, low_ref = refs[:2]
    outs = refs[-2:] if last else refs[-1:]
    total = None
    for place, piece in enumerate(refs[2 : -len(outs)], first):
        size = piece.shape[0]
        modes = slice(place * size, (place + 1) * size)
        high, low = halves(piece[...])
        product = dot(high_ref[:, modes], jnp.concatenate([high, low], axis=1))
        middle = product.shape[1] // 2
        product = product[:, :middle] + (product[:, middle:] + dot(low_ref[:, modes], high))
        total = product if total is None else total + product
    rows = total.shape[0] // 2
    real, imag = [], []
    start = 0
    for width in widths:
        middle, end = start + width, start + 2 * width
        real.append(total[:rows, start:middle] - total[rows:, middle:end])
        imag.append(total[:rows, middle:end] + total[rows:, start:middle])
        start = end
    real, imag = jnp.concatenate(real, axis=1), jnp.concatenate(imag, axis=1)
    if has_total:
        real, imag = real + total_ref[0], imag + total_ref[1]
    if last:
        first_core = core_ref[0] == 0
        real, imag = packed(real), packed(imag)
        outs[0][...] = jnp.where(first_core, real, imag)
        outs[1][...] = jnp.where(first_core, imag, real)
    else:
        outs[0][0], outs[0][1] = real, imag


def add_fields(matrix, pieces, first, widths, core, total=None, last=False):
    rows = matrix[0].shape[0] // 2
    size, width = pieces[0].shape[0], sum(widths)
    shape = packed_shape(rows, width) if last else (2, rows, width)
    out = jax.ShapeDtypeStruct(shape, jnp.float32)
    totals = [] if total is None else [total]
    count = len(pieces)
    return pl.pallas_call(
        functools.partial(fields_kernel, first, widths, total is not None, last),
        in_specs=[SMEM] + [VMEM] * (len(totals) + 2 + count),
        out_specs=[VMEM, VMEM] if last else VMEM,
        out_shape=[out, out] if last else out,
        compiler_params=params(12),
        cost_estimate=COST,
    )(core, *totals, *matrix, *pieces)


def residual(core_ref, kept_ref, other_ref, measured_ref, scale):
    first_core = core_ref[0] == 0
    rows = measured_ref.shape[0]
    kept, other = unpacked(kept_ref[...], rows), unpacked(other_ref[...], rows)
    real, imag = jnp.where(first_core, kept, other), jnp.where(first_core, other, kept)
    excess = real * real + imag * imag - measured_ref[...]
    real, imag = excess * real * scale, excess * imag * scale
    above, below = [], []
    for start, end in groups(0, real.shape[1]):
        above += [real[:, start:end], imag[:, start:end]]
        below += [imag[:, start:end], -real[:, start:end]]
    return jnp.concatenate(
        [jnp.concatenate(above, axis=1), jnp.concatenate(below, axis=1)], axis=0
    )


def gradient_tiles(scale, core_ref, sums, pieces):
    high, low = halves(residual(core_ref, *sums, scale))
    left = jnp.concatenate([high, high, low], axis=1)
    for place, piece in enumerate(pieces):
        high, low = halves(piece[...])
        product = dot(left, jnp.concatenate([high, low, high], axis=1), 1)
        size = product.shape[1]
        yield product.reshape(2, -1, size), slice(place * size, (place + 1) * size)


def part_kernel(scale, parts, core_ref, *refs):
    out_ref = refs[-1]
    sums, pieces = refs[parts : parts + 3], refs[parts + 3 : -1]
    tiles = [
        part_ref.at[:, :, pl.ds(first, pieces[0].shape[0])]
        for part_ref in refs[:parts]
        for first in range(0, part_ref.shape[2], pieces[0].shape[0])
    ]
    for place, (product, modes) in enumerate(gradient_tiles(scale, core_ref, sums, pieces)):
        out_ref[:, :, modes] = product + tiles[place][...] if parts else product


def gradient_part(core, sums, pieces, count, parts=()):
    operands = [*parts, *sums, *pieces]
    modes = len(pieces) * pieces[0].shape[0]
    return pl.pallas_call(
        functools.partial(part_kernel, 1.0 / count, len(parts)),
        in_specs=[SMEM] + [VMEM] * len(operands),
        out_specs=VMEM,
        out_shape=jax.ShapeDtypeStruct((2, sums[-1].shape[0], modes), jnp.float32),
        compiler_params=params(12),
        cost_estimate=COST,
    )(core, *operands)


def last_kernel(scale, core_ref, order_ref, part_ref, *refs):
    pieces, (out_ref, slots_ref, done_ref) = refs[3:-3], refs[-3:]
    copies = []
    for product, modes in gradient_tiles(scale, core_ref, refs[:3], pieces):
        slot, size = len(copies), product.shape[2]
        slots_ref[slot] = product + part_ref[:, :, modes]
        column = pl.multiple_of(order_ref[slot] * size, size)
        copies.append(
            pltpu.make_async_copy(
                slots_ref.at[slot], out_ref.at[:, :, pl.ds(column, size)], done_ref.at[slot]
            )
        )
        copies[-1].start()
    for copy in copies:
        copy.wait()


def last_gradient(core, order, part, sums, pieces, count):
    operands = [part, *sums, *pieces]
    slots = (len(pieces), 2, part.shape[1], pieces[0].shape[0])
    return pl.pallas_call(
        functools.partial(last_kernel, 1.0 / count),
        in_specs=[SMEM, SMEM] + [VMEM] * len(operands),
        out_specs=pl.BlockSpec(memory_space=pl.ANY),
        out_shape=jax.ShapeDtypeStruct(part.shape, jnp.float32),
        scratch_shapes=[pltpu.VMEM(slots, jnp.float32), pltpu.SemaphoreType.DMA(slots[:1])],
        compiler_params=params(20),
        cost_estimate=COST,
    )(core, order, *operands)


def exchange(value, axis, size, mask):
    return lax.ppermute(value, axis, [(i, i ^ mask) for i in range(size)])


def mode_exchange(value, modes, mask):
    return exchange(value, "mode", modes, mask)


def square_body(row_size, mode_size, transfer_matrix, probes, intensity):
    half, count = probes.shape[1] // 2, probes.shape[2]
    row = lax.axis_index("row")
    core = (lax.axis_index("mode") % 2).astype(jnp.int32)[None]
    near = [(0, 0), (0, 1), (1, 0), (2, 1)]
    side = [(1, 1), (2, 0)]
    far = [(3, 0), (3, 1)]
    order = jnp.stack([(row ^ mask) * 2 + which for mask, which in near + side + far]).astype(jnp.int32)

    links = {
        1: [((0, 0), (1, 0)), ((0, 1), (1, 1)), ((2, 1), (3, 1))],
        2: [((0, 1), (2, 1)), ((0, 0), (2, 0)), ((1, 0), (3, 0))],
    }
    cut = count - 2 * LAST_PROBES
    spans = [(0, cut)] if cut else []
    spans += [(cut, cut + LAST_PROBES), (cut + LAST_PROBES, count)]
    ended = {1: [], 2: []}

    def send(chunk, step, *earlier):
        for mask, transfers in links.items():
            source, target = transfers[step]
            value = in_order(chunk[source], *ended[mask][-2:-1], *earlier)
            chunk[target] = exchange(value, "row", row_size, mask)
            ended[mask].append(chunk[target])

    def fields(chunk, places, first, **options):
        pieces = [chunk[place] for place in places]
        return add_fields(matrix, pieces, first, widths, core, **options)

    transfer_matrix = pltpu.with_memory_space_constraint(transfer_matrix, pltpu.HBM)
    probes = pltpu.with_memory_space_constraint(probes, pltpu.HBM)
    chunks = [dict(zip(near[:2], probe_chunk(probes, *span))) for span in spans]
    matrix = matrix_halves(transfer_matrix, order, half)
    places = near + side + far
    bits = [1 << bit for bit in range(1, mode_size.bit_length() - 1)]
    sums, waits, parts = [], [], []

    def tied(chunk, places, *earlier):
        for place in places:
            chunk[place] = in_order(chunk[place], *earlier)

    def first_part(places, *earlier):
        if cut:
            before = in_order(sums[0][0], *earlier), *sums[0][1:]
            pieces = [chunks[0][place] for place in places]
            parts.append(gradient_part(core, before, pieces, count))

    for c, (low, high) in enumerate(spans):
        chunk, widths = chunks[c], group_widths(low, high)
        last = c == len(spans) - 1
        send(chunk, 0, *waits)
        send(chunk, 1, *(sums[-1:] if c else []))
        if last:
            first_part(near, sums[-1])
            total = in_order(sums[-1], *(chunk[place] for place in near[2:]), *parts)
            arrived = mode_exchange(total, mode_size, bits[0])
            near_total = fields(chunk, near, 0)
            total = total + in_order(arrived, near_total)
            send(chunk, 2, *parts)
            first_part(side + far, near_total)
            for mask in bits[1:]:
                total = total + in_order(mode_exchange(total, mode_size, mask), *parts)
            tied(chunk, side, total)
            side_total = fields(chunk, side, len(near), total=near_total)
        else:
            near_total = fields(chunk, near, 0)
            if c:
                total = in_order(sums[-1], near_total)
                total = total + mode_exchange(total, mode_size, bits[0])
                tied(chunk, side, total)
            send(chunk, 2, *([near_total] if c else matrix))
            side_total = fields(chunk, side, len(near), total=near_total)
            if c:
                total = in_order(total, side_total)
                for mask in bits[1:]:
                    total = total + mode_exchange(total, mode_size, mask)
        if c:
            other = mode_exchange(total, mode_size, 1)
            tied(chunk, far, total)
            sums[-1] = total, other, intensity[:, slice(*spans[c - 1])]
        kept, sent = fields(chunk, far, len(near + side), total=side_total, last=True)
        waits = [side_total, *(chunks[c + 1][place] for place in near[:2])] if not last else []
        sums.append(kept + mode_exchange(sent, mode_size, 1))
    arrived = [mode_exchange(sums[-1], mode_size, mask) for mask in (2, *range(mode_size - 2, 2, -2))]
    pieces = [[chunk[place] for place in places] for chunk in chunks[-2:]]
    before = in_order(sums[-2][0], sums[-1]), *sums[-2][1:]
    part = gradient_part(core, before, pieces[0], count, parts)
    total = sum((in_order(value, part) for value in arrived), sums[-1])
    sums[-1] = total, mode_exchange(total, mode_size, 1), intensity[:, slice(*spans[-1])]
    return last_gradient(core, order, part, sums[-1], pieces[1], count)


def plain_body(transfer_matrix, probes, intensity):
    dot = functools.partial(
        jnp.einsum, precision=lax.Precision.HIGHEST, preferred_element_type=jnp.float32
    )
    strip = lax.all_gather(probes, "row", axis=1, tiled=True)
    products = dot("amn,bnp->abmp", transfer_matrix, strip)
    fields = jnp.stack([products[0, 0] - products[1, 1], products[0, 1] + products[1, 0]])
    fields = lax.psum(fields, "mode")
    excess = fields[0] * fields[0] + fields[1] * fields[1] - intensity
    residual = excess[None] * fields / probes.shape[2]
    products = dot("amp,bnp->abmn", residual, strip)
    return jnp.stack([products[0, 0] + products[1, 1], products[1, 0] - products[0, 1]])


def solution(mesh):
    in_specs = (P(None, "row", "mode"), P(None, ("mode", "row"), None), P("row", None))
    out_specs = P(None, "row", "mode")
    row_size, mode_size = mesh.shape["row"], mesh.shape["mode"]

    def body(transfer_matrix, probes, intensity):
        square = (
            row_size == 4
            and mode_size & (mode_size - 1) == 0
            and mode_size > 2
            and probes.shape[1] % (2 * LANES) == 0
            and probes.shape[2] % LANES == 0
            and probes.shape[2] >= 2 * LAST_PROBES
            and transfer_matrix.shape[1] % 16 == 0
        )
        if square:
            return square_body(row_size, mode_size, transfer_matrix, probes, intensity)
        return plain_body(transfer_matrix, probes, intensity)

    return jax.shard_map(body, mesh=mesh, in_specs=in_specs, out_specs=out_specs, check_vma=False)
```

```python
import functools

import jax
import jax.numpy as jnp
from jax import lax
from jax.experimental import pallas as pl
from jax.experimental.pallas import tpu as pltpu
from jax.sharding import PartitionSpec as P

LANES = 128
LAST_PROBES = 64
MIB = 1024 * 1024
VMEM = pl.BlockSpec(memory_space=pltpu.VMEM)
SMEM = pl.BlockSpec(memory_space=pltpu.SMEM)
COST = pl.CostEstimate(flops=1000, bytes_accessed=1000, transcendentals=0)


def halves(value):
    high = value.astype(jnp.bfloat16)
    return high, (value - high.astype(jnp.float32)).astype(jnp.bfloat16)


def dot(left, right, dimension=0):
    return lax.dot_general(
        left, right, (((1,), (dimension,)), ((), ())), preferred_element_type=jnp.float32
    )


def params(mib):
    return pltpu.CompilerParams(vmem_limit_bytes=mib * MIB)


def in_order(value, *earlier):
    return lax.optimization_barrier((value, *earlier))[0]


def groups(low, high):
    cuts = [low, *range(low // LANES * LANES + LANES, high, LANES), high]
    return list(zip(cuts, cuts[1:]))


def group_widths(low, high):
    return [end - start for start, end in groups(low, high)]


def chunk_kernel(low, high, probes_ref, *refs):
    outs, (slots_ref, done_ref, slot_done_ref) = refs[:2], refs[2:]
    half = outs[0].shape[0]
    copies, later = [], []
    for which, out_ref in enumerate(outs):
        place = 0
        modes = pl.ds(which * half, half)
        for start, end in groups(low, high):
            block = pl.ds(start // LANES * LANES, LANES)
            for part in range(2):
                if end - start == LANES:
                    target = out_ref.at[:, pl.ds(place + part * LANES, LANES)]
                    copy = pltpu.make_async_copy(
                        probes_ref.at[part, modes, block], target, done_ref.at[len(copies)]
                    )
                    copies.append(copy)
                else:
                    slot = 2 * which + part
                    copy = pltpu.make_async_copy(
                        probes_ref.at[part, modes, block], slots_ref.at[slot], slot_done_ref.at[slot]
                    )
                    later.append((copy, out_ref, slot, place + part * (end - start), start, end))
                copy.start()
            place += 2 * (end - start)
    for copy, out_ref, slot, place, start, end in later:
        copy.wait()
        first = start % LANES
        out_ref[:, place : place + end - start] = slots_ref[slot, :, first : first + end - start]
    for copy in copies:
        copy.wait()


def probe_chunk(probes, low, high):
    half, width = probes.shape[1] // 2, high - low
    whole = sum(size == LANES for size in group_widths(low, high))
    return pl.pallas_call(
        functools.partial(chunk_kernel, low, high),
        in_specs=[pl.BlockSpec(memory_space=pl.ANY)],
        out_specs=[VMEM, VMEM],
        out_shape=[jax.ShapeDtypeStruct((half, 2 * width), jnp.float32)] * 2,
        scratch_shapes=[
            pltpu.VMEM((4, half, LANES), jnp.float32),
            pltpu.SemaphoreType.DMA((max(4 * whole, 1),)),
            pltpu.SemaphoreType.DMA((4,)),
        ],
        compiler_params=params(8),
        cost_estimate=COST,
    )(probes)


def matrix_kernel(order_ref, matrix_ref, high_ref, low_ref):
    high_ref[...], low_ref[...] = halves(matrix_ref[...].reshape(high_ref.shape))


def matrix_halves(matrix, order, half):
    _, rows, modes = matrix.shape
    out = jax.ShapeDtypeStruct((2 * rows, modes), jnp.bfloat16)
    spec = pl.BlockSpec((2 * rows, half), lambda i, _: (0, i))
    return pl.pallas_call(
        matrix_kernel,
        grid_spec=pltpu.PrefetchScalarGridSpec(
            num_scalar_prefetch=1,
            grid=(modes // half,),
            in_specs=[pl.BlockSpec((2, rows, half), lambda i, order_ref: (0, 0, order_ref[i]))],
            out_specs=[spec, spec],
        ),
        out_shape=[out, out],
        compiler_params=params(12),
        cost_estimate=COST,
    )(order, matrix)


def packed_shape(rows, width):
    return rows * width // LANES, LANES


def packed(value):
    rows, width = value.shape
    blocks = [value[:, i : i + LANES] for i in range(0, width, LANES)]
    left = blocks[-1].shape[1]
    if left < LANES:
        fold = rows * left // LANES
        blocks[-1] = jnp.concatenate(
            [blocks[-1][i : i + fold] for i in range(0, rows, fold)], axis=1
        )
    return jnp.concatenate(blocks, axis=0)


def unpacked(value, rows):
    whole, left = divmod(value.shape[0], rows)
    blocks = [value[i * rows : (i + 1) * rows] for i in range(whole)]
    if left:
        width = left * LANES // rows
        folded = value[whole * rows :]
        blocks.append(
            jnp.concatenate([folded[:, i : i + width] for i in range(0, LANES, width)], axis=0)
        )
    return jnp.concatenate(blocks, axis=1)


def fields_kernel(first, widths, has_total, last, *refs):
    refs = list(refs)
    core_ref = refs.pop(0)
    total_ref = refs.pop(0) if has_total else None
    high_ref, low_ref = refs[:2]
    outs = refs[-2:] if last else refs[-1:]
    total = None
    for place, piece in enumerate(refs[2 : -len(outs)], first):
        size = piece.shape[0]
        modes = slice(place * size, (place + 1) * size)
        high, low = halves(piece[...])
        product = dot(high_ref[:, modes], jnp.concatenate([high, low], axis=1))
        middle = product.shape[1] // 2
        product = product[:, :middle] + (product[:, middle:] + dot(low_ref[:, modes], high))
        total = product if total is None else total + product
    rows = total.shape[0] // 2
    real, imag = [], []
    start = 0
    for width in widths:
        middle, end = start + width, start + 2 * width
        real.append(total[:rows, start:middle] - total[rows:, middle:end])
        imag.append(total[:rows, middle:end] + total[rows:, start:middle])
        start = end
    real, imag = jnp.concatenate(real, axis=1), jnp.concatenate(imag, axis=1)
    if has_total:
        real, imag = real + total_ref[0], imag + total_ref[1]
    if last:
        first_core = core_ref[0] == 0
        real, imag = packed(real), packed(imag)
        outs[0][...] = jnp.where(first_core, real, imag)
        outs[1][...] = jnp.where(first_core, imag, real)
    else:
        outs[0][0], outs[0][1] = real, imag


def add_fields(matrix, pieces, first, widths, core, total=None, last=False):
    rows = matrix[0].shape[0] // 2
    size, width = pieces[0].shape[0], sum(widths)
    shape = packed_shape(rows, width) if last else (2, rows, width)
    out = jax.ShapeDtypeStruct(shape, jnp.float32)
    totals = [] if total is None else [total]
    count = len(pieces)
    return pl.pallas_call(
        functools.partial(fields_kernel, first, widths, total is not None, last),
        in_specs=[SMEM] + [VMEM] * (len(totals) + 2 + count),
        out_specs=[VMEM, VMEM] if last else VMEM,
        out_shape=[out, out] if last else out,
        compiler_params=params(12),
        cost_estimate=COST,
    )(core, *totals, *matrix, *pieces)


def residual(core_ref, kept_ref, other_ref, measured_ref, scale):
    first_core = core_ref[0] == 0
    rows = measured_ref.shape[0]
    kept, other = unpacked(kept_ref[...], rows), unpacked(other_ref[...], rows)
    real, imag = jnp.where(first_core, kept, other), jnp.where(first_core, other, kept)
    excess = real * real + imag * imag - measured_ref[...]
    real, imag = excess * real * scale, excess * imag * scale
    above, below = [], []
    for start, end in groups(0, real.shape[1]):
        above += [real[:, start:end], imag[:, start:end]]
        below += [imag[:, start:end], -real[:, start:end]]
    return jnp.concatenate(
        [jnp.concatenate(above, axis=1), jnp.concatenate(below, axis=1)], axis=0
    )


def gradient_tiles(scale, core_ref, sums, pieces):
    high, low = halves(residual(core_ref, *sums, scale))
    left = jnp.concatenate([high, high, low], axis=1)
    for place, piece in enumerate(pieces):
        high, low = halves(piece[...])
        product = dot(left, jnp.concatenate([high, low, high], axis=1), 1)
        size = product.shape[1]
        yield product.reshape(2, -1, size), slice(place * size, (place + 1) * size)


def part_kernel(scale, parts, core_ref, *refs):
    out_ref = refs[-1]
    sums, pieces = refs[parts : parts + 3], refs[parts + 3 : -1]
    tiles = [
        part_ref.at[:, :, pl.ds(first, pieces[0].shape[0])]
        for part_ref in refs[:parts]
        for first in range(0, part_ref.shape[2], pieces[0].shape[0])
    ]
    for place, (product, modes) in enumerate(gradient_tiles(scale, core_ref, sums, pieces)):
        out_ref[:, :, modes] = product + tiles[place][...] if parts else product


def gradient_part(core, sums, pieces, count, parts=()):
    operands = [*parts, *sums, *pieces]
    modes = len(pieces) * pieces[0].shape[0]
    return pl.pallas_call(
        functools.partial(part_kernel, 1.0 / count, len(parts)),
        in_specs=[SMEM] + [VMEM] * len(operands),
        out_specs=VMEM,
        out_shape=jax.ShapeDtypeStruct((2, sums[-1].shape[0], modes), jnp.float32),
        compiler_params=params(12),
        cost_estimate=COST,
    )(core, *operands)


def last_kernel(scale, core_ref, order_ref, part_ref, *refs):
    pieces, (out_ref, slots_ref, done_ref) = refs[3:-3], refs[-3:]
    copies = []
    for product, modes in gradient_tiles(scale, core_ref, refs[:3], pieces):
        slot, size = len(copies), product.shape[2]
        slots_ref[slot] = product + part_ref[:, :, modes]
        column = pl.multiple_of(order_ref[slot] * size, size)
        copies.append(
            pltpu.make_async_copy(
                slots_ref.at[slot], out_ref.at[:, :, pl.ds(column, size)], done_ref.at[slot]
            )
        )
        copies[-1].start()
    for copy in copies:
        copy.wait()


def last_gradient(core, order, part, sums, pieces, count):
    operands = [part, *sums, *pieces]
    slots = (len(pieces), 2, part.shape[1], pieces[0].shape[0])
    return pl.pallas_call(
        functools.partial(last_kernel, 1.0 / count),
        in_specs=[SMEM, SMEM] + [VMEM] * len(operands),
        out_specs=pl.BlockSpec(memory_space=pl.ANY),
        out_shape=jax.ShapeDtypeStruct(part.shape, jnp.float32),
        scratch_shapes=[pltpu.VMEM(slots, jnp.float32), pltpu.SemaphoreType.DMA(slots[:1])],
        compiler_params=params(20),
        cost_estimate=COST,
    )(core, order, *operands)


def exchange(value, axis, size, mask):
    return lax.ppermute(value, axis, [(i, i ^ mask) for i in range(size)])


def mode_exchange(value, modes, mask):
    return exchange(value, "mode", modes, mask)


def square_body(row_size, mode_size, transfer_matrix, probes, intensity):
    half, count = probes.shape[1] // 2, probes.shape[2]
    row = lax.axis_index("row")
    core = (lax.axis_index("mode") % 2).astype(jnp.int32)[None]
    near = [(0, 0), (0, 1), (1, 0), (2, 1)]
    side = [(1, 1), (2, 0)]
    far = [(3, 0), (3, 1)]
    order = jnp.stack([(row ^ mask) * 2 + which for mask, which in near + side + far]).astype(jnp.int32)

    links = {
        1: [((0, 0), (1, 0)), ((0, 1), (1, 1)), ((2, 1), (3, 1))],
        2: [((0, 1), (2, 1)), ((0, 0), (2, 0)), ((1, 0), (3, 0))],
    }
    cut = count - 2 * LAST_PROBES
    spans = [(0, cut)] if cut else []
    spans += [(cut, cut + LAST_PROBES), (cut + LAST_PROBES, count)]
    ended = {1: [], 2: []}

    def send(chunk, step, *earlier):
        for mask, transfers in links.items():
            source, target = transfers[step]
            value = in_order(chunk[source], *ended[mask][-2:-1], *earlier)
            chunk[target] = exchange(value, "row", row_size, mask)
            ended[mask].append(chunk[target])

    def fields(chunk, places, first, **options):
        pieces = [chunk[place] for place in places]
        return add_fields(matrix, pieces, first, widths, core, **options)

    transfer_matrix = pltpu.with_memory_space_constraint(transfer_matrix, pltpu.HBM)
    probes = pltpu.with_memory_space_constraint(probes, pltpu.HBM)
    chunks = [dict(zip(near[:2], probe_chunk(probes, *span))) for span in spans]
    matrix = matrix_halves(transfer_matrix, order, half)
    places = near + side + far
    bits = [1 << bit for bit in reversed(range(1, mode_size.bit_length() - 1))]
    sums, waits, parts = [], [], []

    def tied(chunk, places, *earlier):
        for place in places:
            chunk[place] = in_order(chunk[place], *earlier)

    def first_part(places, *earlier):
        if cut:
            before = in_order(sums[0][0], *earlier), *sums[0][1:]
            pieces = [chunks[0][place] for place in places]
            parts.append(gradient_part(core, before, pieces, count))

    for c, (low, high) in enumerate(spans):
        chunk, widths = chunks[c], group_widths(low, high)
        last = c == len(spans) - 1
        send(chunk, 0, *waits)
        send(chunk, 1, *(sums[-1:] if c else []))
        if last:
            first_part(near, sums[-1])
            total = in_order(sums[-1], *(chunk[place] for place in near[2:]), *parts)
            arrived = mode_exchange(total, mode_size, bits[0])
            near_total = fields(chunk, near, 0)
            total = total + in_order(arrived, near_total)
            send(chunk, 2, *parts)
            first_part(side + far, near_total)
            for mask in bits[1:]:
                total = total + in_order(mode_exchange(total, mode_size, mask), *parts)
            tied(chunk, side, total)
            side_total = fields(chunk, side, len(near), total=near_total)
        else:
            near_total = fields(chunk, near, 0)
            if c:
                total = in_order(sums[-1], near_total)
                total = total + mode_exchange(total, mode_size, bits[0])
                tied(chunk, side, total)
            send(chunk, 2, *([near_total] if c else matrix))
            side_total = fields(chunk, side, len(near), total=near_total)
            if c:
                total = in_order(total, side_total)
                for mask in bits[1:]:
                    total = total + mode_exchange(total, mode_size, mask)
        if c:
            other = mode_exchange(total, mode_size, 1)
            tied(chunk, far, total, *([other] if last else []))
            sums[-1] = total, other, intensity[:, slice(*spans[c - 1])]
        kept, sent = fields(chunk, far, len(near + side), total=side_total, last=True)
        waits = [side_total, *(chunks[c + 1][place] for place in near[:2])] if not last else []
        sums.append(kept + mode_exchange(sent, mode_size, 1))
    arrived = [mode_exchange(sums[-1], mode_size, mask) for mask in (2, *range(mode_size - 2, 2, -2))]
    pieces = [[chunk[place] for place in places] for chunk in chunks[-2:]]
    before = in_order(sums[-2][0], sums[-1]), *sums[-2][1:]
    part = gradient_part(core, before, pieces[0], count, parts)
    total = sum((in_order(value, part) for value in arrived), sums[-1])
    sums[-1] = total, mode_exchange(total, mode_size, 1), intensity[:, slice(*spans[-1])]
    return last_gradient(core, order, part, sums[-1], pieces[1], count)


def plain_body(transfer_matrix, probes, intensity):
    dot = functools.partial(
        jnp.einsum, precision=lax.Precision.HIGHEST, preferred_element_type=jnp.float32
    )
    strip = lax.all_gather(probes, "row", axis=1, tiled=True)
    products = dot("amn,bnp->abmp", transfer_matrix, strip)
    fields = jnp.stack([products[0, 0] - products[1, 1], products[0, 1] + products[1, 0]])
    fields = lax.psum(fields, "mode")
    excess = fields[0] * fields[0] + fields[1] * fields[1] - intensity
    residual = excess[None] * fields / probes.shape[2]
    products = dot("amp,bnp->abmn", residual, strip)
    return jnp.stack([products[0, 0] + products[1, 1], products[1, 0] - products[0, 1]])


def solution(mesh):
    in_specs = (P(None, "row", "mode"), P(None, ("mode", "row"), None), P("row", None))
    out_specs = P(None, "row", "mode")
    row_size, mode_size = mesh.shape["row"], mesh.shape["mode"]

    def body(transfer_matrix, probes, intensity):
        square = (
            row_size == 4
            and mode_size & (mode_size - 1) == 0
            and mode_size > 1
            and probes.shape[1] % (2 * LANES) == 0
            and probes.shape[2] % LANES == 0
            and probes.shape[2] >= 2 * LAST_PROBES
            and transfer_matrix.shape[1] % 16 == 0
        )
        if square:
            return square_body(row_size, mode_size, transfer_matrix, probes, intensity)
        return plain_body(transfer_matrix, probes, intensity)

    return jax.shard_map(body, mesh=mesh, in_specs=in_specs, out_specs=out_specs, check_vma=False)
```
